128 devices in a mesh: pool: 2 (over x_lo), pw: 64 (over z, x_hi, y, core).
Axes of the slice: x: 4 (x_hi: 2, x_lo: 2; x = x_hi * 2 + x_lo), y: 4, z: 4, core: 2. Of those that a mesh axis runs over, the one named last changes fastest.
Arguments:
- orbitals: float32 [2, 2, 2, 192, 192, 192], P('pool', None, None, 'pw'), may hold values from -6 to 6
- responses: float32 [2, 2, 2, 192, 192, 192], P('pool', None, None, 'pw'), may hold values from -6 to 6
- energies: float32 [2, 2], P('pool'), may hold values from -0.6 to 0.4
- weights: float32 [2], P('pool'), may hold values from 0.5 to 1.5
- potential: float32 [192, 192, 192], P(None, 'pw'), may hold values from -3 to 3
- perturbation: float32 [192, 192, 192], P(None, 'pw'), may hold values from 0.2 to 2
Outputs:
- new_responses: float32 [2, 2, 2, 192, 192, 192], P('pool', None, None, 'pw')
- response_density: float32 [192, 192, 192], P('pw')
The draws below stay inside these ranges and needn't reach their ends.
All inputs are finite; a program needn't handle non-finite values.
Results may differ from the reference program's by a relative error of at most 0.0003.
Values sent between devices are 32-bit elements; how exact they have to be, the bound alone decides.
A program may use at most 128 MiB of HBM per device.

```python
import jax
import jax.numpy as jnp
from jax import lax

GRID = 192
BANDS = 2
KPTS = 2


def block_scale(own_key, dims, cuts, low, top_value):
    factor_of = 1.0
    for position, shards_of in cuts:
        draws = jax.random.uniform(jax.random.fold_in(jax.random.fold_in(own_key, 6), position), (shards_of,), jnp.float32, low / len(cuts), top_value / len(cuts))
        factor_of = factor_of * jnp.repeat(jnp.exp(draws), dims[position] // shards_of).reshape((-1,) + (1,) * (len(dims) - 1 - position))
    return factor_of


def scatter_about(own_key, dims, spread, limit, shards=(), held_as=jnp.bfloat16):
    entries = spread * jax.random.normal(own_key, dims, jnp.float32)
    if shards:
        entries = entries * block_scale(own_key, dims, shards, -0.22, 0.18)
    return jnp.clip(entries, -limit, limit).astype(held_as)


def setup_inputs(seed: int = 0) -> dict:
    streams_of = jax.random.split(jax.random.key(seed), 7)
    return {
        "orbitals": scatter_about(streams_of[0], (KPTS, BANDS, 2, GRID, GRID, GRID), 1.0, 6.0, ((0, 2), (3, 64)), jnp.float32),
        "responses": scatter_about(streams_of[1], (KPTS, BANDS, 2, GRID, GRID, GRID), 1.0, 6.0, ((0, 2), (3, 64)), jnp.float32),
        "energies": jnp.clip(-0.6 + 1 * jax.random.uniform(streams_of[2], (KPTS, BANDS), jnp.float32) ** block_scale(streams_of[2], (KPTS, BANDS), ((0, 2),), -0.2, 0.2), -0.6, 0.4),
        "weights": jnp.clip(0.5 + 1.0 * jax.random.uniform(streams_of[3], (KPTS,), jnp.float32) ** block_scale(streams_of[3], (KPTS,), ((0, 2),), -0.2, 0.2), 0.5, 1.5),
        "potential": jnp.clip(jax.random.uniform(streams_of[4], (GRID, GRID, GRID), jnp.float32, -3.0, 3.0) * block_scale(streams_of[4], (GRID, GRID, GRID), ((1, 64),), -0.4, 0.0), -3.0, 3.0),
        "perturbation": jnp.clip(0.2 + 1.8 * jax.random.uniform(streams_of[5], (GRID, GRID, GRID), jnp.float32) ** block_scale(streams_of[5], (GRID, GRID, GRID), ((1, 64),), -0.2, 0.2), 0.2, 2.0),
    }


RECIPROCAL_SQUARE = 0.023428
ORDERINGS = ((0, 1, 2), (1, 0, 2))


def negated(values, along_axis):
    return jnp.roll(jnp.flip(values, along_axis), 1, along_axis)


def reference(orbitals, responses, energies, weights, potential, perturbation):
    length = orbitals.shape[-1]
    frequency = jnp.arange(length, dtype=jnp.int32)
    frequency = jnp.where(frequency < length // 2, frequency, frequency - length).astype(jnp.float32)
    kinetic = 0.5 * RECIPROCAL_SQUARE * (frequency[:, None, None] * frequency[:, None, None] + frequency[None, :, None] * frequency[None, :, None] + frequency[None, None, :] * frequency[None, None, :])
    cell_count = float(length ** 3)
    density = jnp.zeros((length, length, length), jnp.float32)
    updated_all = []
    for kpoint in range(KPTS):
        residual_list = []
        for band_index in range(BANDS):
            orbital_space = jnp.fft.ifftn(lax.complex(orbitals[kpoint, band_index, 0], orbitals[kpoint, band_index, 1]), norm="ortho")
            response_space = jnp.fft.ifftn(lax.complex(responses[kpoint, band_index, 0], responses[kpoint, band_index, 1]), norm="ortho")
            density = density + 2.0 * weights[kpoint] * (orbital_space.real * response_space.real + orbital_space.imag * response_space.imag)
            applied_space = potential * response_space + perturbation * orbital_space
            applied = jnp.fft.fftn(applied_space, norm="ortho")
            shifted = kinetic - energies[kpoint, band_index]
            residual_real = shifted * responses[kpoint, band_index, 0] + applied.real
            residual_imag = shifted * responses[kpoint, band_index, 1] + applied.imag
            residual_list.append(jnp.stack((residual_real, residual_imag)))
        residual = jnp.stack(residual_list)
        left_real = orbitals[kpoint, :, 0].reshape(BANDS, -1)
        left_imag = orbitals[kpoint, :, 1].reshape(BANDS, -1)
        right_real = residual[:, 0].reshape(BANDS, -1)
        right_imag = residual[:, 1].reshape(BANDS, -1)
        highest = lax.Precision.HIGHEST
        over_real = jnp.dot(left_real, right_real.T, precision=highest) + jnp.dot(left_imag, right_imag.T, precision=highest)
        over_imag = jnp.dot(left_real, right_imag.T, precision=highest) - jnp.dot(left_imag, right_real.T, precision=highest)
        combine_real = jnp.dot(over_real.T, left_real, precision=highest) - jnp.dot(over_imag.T, left_imag, precision=highest)
        combine_imag = jnp.dot(over_imag.T, left_real, precision=highest) + jnp.dot(over_real.T, left_imag, precision=highest)
        combined = jnp.stack((combine_real, combine_imag), axis=1).reshape(residual.shape)
        projected = residual - combined / cell_count
        updated_all.append(responses[kpoint] - projected / (1.0 + kinetic))
    new_responses = jnp.stack(updated_all)
    summed = jnp.zeros_like(density)
    for pattern in range(4):
        flipped = density
        for along_axis in range(2):
            if (pattern >> along_axis) & 1:
                flipped = negated(flipped, along_axis)
        for ordering in ORDERINGS:
            summed = summed + jnp.transpose(flipped, ordering)
    return new_responses, summed / 8.0
```

```python
import functools
import math

import jax
import jax.numpy as jnp
import ml_dtypes
import numpy as np
from jax import lax
from jax.experimental import pallas as pl
from jax.experimental.pallas import tpu as pltpu
from jax.sharding import PartitionSpec as P

RECIPROCAL_SQUARE = 0.023428
G = 192
W = 64
R = 3
H = 104
BLOCKS = 27
MESH = pl.DeviceIdType.MESH
F32 = jnp.float32
BF16 = jnp.bfloat16


def halves(table):
    high = table.astype(ml_dtypes.bfloat16)
    low = (table - high.astype(np.float64)).astype(ml_dtypes.bfloat16)
    return [high, low]


def tables():
    index = np.arange(G)
    angles = (np.outer(index, index) % G) * (2.0 * math.pi / G)
    cosine = np.cos(angles) / math.sqrt(G)
    sine = np.sin(angles) / math.sqrt(G)
    spread = np.array([R * (s % W) + s // W for s in range(G)])

    def packed(left, right):
        return np.concatenate(
            (left[:, :128], right[:, :128], left[:, 128:], right[:, 128:]), axis=1
        )

    out_left = np.concatenate((cosine[spread], sine[spread]), axis=0)
    in_left = np.concatenate((cosine[:, spread], sine[:, spread]), axis=0)
    right_real = packed(cosine, sine)
    right_imag = packed(-sine, cosine)
    back_real = packed(cosine, -sine)
    back_imag = packed(sine, cosine)
    back = np.concatenate(
        (back_real[:128], back_imag[:128], back_real[128:], back_imag[128:]), axis=0
    )
    fold = np.zeros((H, G))
    unfold = np.zeros((G, H))
    merge = np.zeros((G, G))
    expand = np.zeros((G, H))
    for a in range(H):
        fold[a, a] += 1.0
        fold[a, -a % G] += 1.0
    for s in range(G):
        a = spread[s]
        unfold[s, min(a, G - a)] = 1.0
        merge[a, s] += 1.0
        merge[-a % G, s] += 1.0
        expand[s, min(s, G - s)] = 1.0
    held = []
    for table in (right_real, right_imag, out_left, in_left, back):
        held += halves(table)
    return held + [m.astype(ml_dtypes.bfloat16) for m in (fold, unfold, merge, expand)]


def split(values):
    high = values.astype(BF16)
    return high, (values - high.astype(F32)).astype(BF16)


def dot(left, right):
    return jnp.dot(left, right, preferred_element_type=F32)


def table_left(high, low, values):
    top, rest = split(values)
    return dot(high, top) + (dot(high, rest) + dot(low, top))


def table_right(values, high, low):
    top, rest = split(values)
    return dot(top, high) + (dot(rest, high) + dot(top, low))


def exact_left(table, values):
    top, rest = split(values)
    last = (values - top.astype(F32) - rest.astype(F32)).astype(BF16)
    return dot(table, top) + (dot(table, rest) + dot(table, last))


def swap64(values):
    return pltpu.roll(values, 64, axis=1)


def lane_sign():
    return jnp.where(lax.broadcasted_iota(jnp.int32, (1, 128), 1) < 64, -1.0, 1.0).astype(F32)


def spin(product, sign):
    cos_part, sin_part = product[:G], product[G:]
    return (
        cos_part[:, :128] - sign * sin_part[:, 128:256],
        cos_part[:, 128:256] + sign * sin_part[:, :128],
        cos_part[:, 256:] + (sign * lane_sign()) * swap64(sin_part[:, 256:]),
    )


def rows_of(start, count):
    return pl.ds(pl.multiple_of(start, 8), count)


def tiles_at(view, start):
    return jnp.concatenate([view[rows_of(start + t * G, G), :] for t in range(3)], axis=1)


def row_sums(values):
    total = values[0:8]
    for s in range(8, G, 8):
        total = total + values[s : s + 8]
    return total


def squared_freq(index):
    freq = jnp.where(index < G // 2, index, index - G).astype(F32)
    return freq * freq


def kinetic_plane(row):
    plane = squared_freq(lax.broadcasted_iota(jnp.int32, (G, G), 0))
    plane = plane + squared_freq(lax.broadcasted_iota(jnp.int32, (G, G), 1))
    return (0.5 * RECIPROCAL_SQUARE) * (squared_freq(row) + plane)


def kernel(
    orb_hbm, resp_hbm, pot_hbm, pert_hbm, energies, weights, *refs
):
    table_hbm = refs[:14]
    new_hbm, dens_hbm = refs[14:16]
    tables_in = refs[16:30]
    (
        raw, pot, pert, out_a, in_a, out_r, in_r, orb_space, app_space, dens,
        fold_mine, fold_other, fold_sum, fold_mirror, spread_out, spread_in,
        sums, sums_g, row_out, row_in, new_buf, dens_buf,
        load_sem, table_sem, send_a, recv_a, send_r, recv_r, send_d, recv_d, store_sem,
    ) = refs[30:]
    (wr_h, wr_l, wi_h, wi_l, ol_h, ol_l, il_h, il_l, bk_h, bk_l, fold, unfold, merge, expand) = tables_in

    me = lax.axis_index("pw")
    pool = lax.axis_index("pool")

    def load_table(k):
        return pltpu.make_async_copy(table_hbm[k], tables_in[k], table_sem.at[k])

    def load_unit(u):
        source = orb_hbm if u % 2 == 0 else resp_hbm
        return pltpu.make_async_copy(source.at[0, u // 2], raw.at[u], load_sem.at[u])

    loads_pot = pltpu.make_async_copy(pot_hbm, pot, load_sem.at[4])
    loads_pert = pltpu.make_async_copy(pert_hbm, pert, load_sem.at[5])
    for k in range(4):
        load_table(k).start()
    load_unit(0).start()
    for k in range(4, 6):
        load_table(k).start()
    for u in range(1, 4):
        load_unit(u).start()
    for k in range(6, 14):
        load_table(k).start()
    loads_pot.start()
    loads_pert.start()

    barrier = pltpu.get_barrier_semaphore()

    def peer_at(k):
        return me ^ (1 + (k * 37 + 11) % (W - 1))

    @pl.loop(0, W - 1)
    def _(k):
        pl.semaphore_signal(barrier, inc=1, device_id={"pw": peer_at(k)}, device_id_type=MESH)

    pl.semaphore_signal(barrier, inc=1, device_id={"pool": 1 - pool}, device_id_type=MESH)

    out_a_rows = out_a.reshape(4 * BLOCKS * W, 128)
    in_a_rows = in_a.reshape(4 * BLOCKS * W, 128)
    out_r_rows = out_r.reshape(2 * BLOCKS * W, 128)
    in_r_rows = in_r.reshape(2 * BLOCKS * W, 128)
    spread_out_rows = spread_out.reshape(15 * W, 128)
    spread_in_rows = spread_in.reshape(15 * W, 128)
    row_in_rows = row_in.reshape(W, 128)

    for k in range(6):
        load_table(k).wait()

    for u in range(4):
        load_unit(u).wait()

        @pl.loop(0, R)
        def _(i):
            planes = table_right(raw[u, 0, i], wr_h[...], wr_l[...]) + table_right(
                raw[u, 1, i], wi_h[...], wi_l[...]
            )
            parts = spin(table_left(ol_h[...], ol_l[...], planes), 1.0)
            for j in range(R):
                for t in range(3):
                    start = (u * BLOCKS + (j * 3 + t) * R + i) * W
                    out_a_rows[rows_of(start, W), :] = parts[t][j * W : (j + 1) * W]

        if u == 0:
            pl.semaphore_wait(barrier, W)

        @pl.loop(0, W - 1)
        def _(k):
            peer = peer_at(k)
            pltpu.make_async_remote_copy(
                src_ref=out_a.at[u, :, peer],
                dst_ref=in_a.at[u, :, me],
                send_sem=send_a.at[u],
                recv_sem=recv_a.at[u],
                device_id={"pw": peer},
                device_id_type=MESH,
            ).start()

        pltpu.make_async_copy(out_a.at[u, :, me], in_a.at[u, :, me], load_sem.at[6 + u]).start()

    for k in range(6, 14):
        load_table(k).wait()

    sums_g[...] = jnp.zeros_like(sums_g)

    @pl.loop(0, R)
    def _(i):
        kinetic = kinetic_plane(R * me + i)
        for n in range(2):
            shifted = kinetic - energies[0, n]
            real = shifted * raw[2 * n + 1, 0, i]
            imag = shifted * raw[2 * n + 1, 1, i]
            for m in range(2):
                left_real, left_imag = raw[2 * m, 0, i], raw[2 * m, 1, i]
                at = (m * 2 + n) * 2
                sums_g[at] += row_sums(left_real * real + left_imag * imag)
                sums_g[at + 1] += row_sums(left_real * imag - left_imag * real)

    loads_pot.wait()
    loads_pert.wait()
    sums[...] = jnp.zeros_like(sums)

    for n in range(2):
        for u in (2 * n, 2 * n + 1):
            landed = in_a.at[u, :, pl.ds(0, W - 1)]
            pltpu.make_async_copy(landed, landed, recv_a.at[u]).wait()
            pltpu.make_async_copy(out_a.at[u, :, me], in_a.at[u, :, me], load_sem.at[6 + u]).wait()

        @pl.loop(0, R)
        def _(j):
            at = j * 3 * G
            first = 2 * n * BLOCKS * W
            second = (2 * n + 1) * BLOCKS * W
            orb = spin(table_left(il_h[...], il_l[...], tiles_at(in_a_rows, first + at)), 1.0)
            resp = spin(table_left(il_h[...], il_l[...], tiles_at(in_a_rows, second + at)), 1.0)
            pot_top = pot[j, :, 0:128]
            pert_top = pert[j, :, 0:128]
            pot_end = jnp.concatenate((pot[j, :, 128:G], pot[j, :, 128:G]), axis=1)
            pert_end = jnp.concatenate((pert[j, :, 128:G], pert[j, :, 128:G]), axis=1)
            app = (
                pot_top * resp[0] + pert_top * orb[0],
                pot_top * resp[1] + pert_top * orb[1],
                pot_end * resp[2] + pert_end * orb[2],
            )
            ends = orb[2] * resp[2]
            density = (2.0 * weights[0]) * jnp.concatenate(
                (orb[0] * resp[0] + orb[1] * resp[1], ends + swap64(ends)), axis=1
            )

            def overlap(left, right, slot):
                sums[slot] += row_sums(left[0] * right[0] + left[1] * right[1] + left[2] * right[2])
                sums[slot + 1] += row_sums(
                    left[0] * right[1]
                    - left[1] * right[0]
                    - lane_sign() * left[2] * swap64(right[2])
                )

            if n == 0:
                overlap(orb, app, 0)
                dens[j] = density
                for t in range(3):
                    orb_space[j, t] = orb[t]
                    app_space[j, t] = app[t]
            else:
                dens[j] = dens[j] + density
                orb_first = [orb_space[j, t] for t in range(3)]
                app_first = [app_space[j, t] for t in range(3)]
                overlap(orb_first, app, 2)
                overlap(orb, app_first, 4)
                overlap(orb, app, 6)
            product = table_left(ol_h[...], ol_l[...], jnp.concatenate(app, axis=1))
            turned = jnp.concatenate(spin(product, -1.0), axis=1)
            back = table_right(turned, bk_h[...], bk_l[...])
            for i in range(R):
                for t in range(3):
                    start = (n * BLOCKS + (i * 3 + t) * R + j) * W
                    out_r_rows[rows_of(start, W), :] = back[
                        i * W : (i + 1) * W, t * 128 : (t + 1) * 128
                    ]

        if n == 1:
            low = lax.broadcasted_iota(jnp.int32, (1, 128), 1) < 64
            strips = (
                dens[0, :, 0:128],
                dens[0, :, 128:256],
                dens[1, :, 0:128],
                dens[2, :, 0:128],
                jnp.where(low, dens[1, :, 128:256], dens[2, :, 128:256]),
            )
            folded = exact_left(fold[...], jnp.concatenate(strips, axis=1))
            for t in range(5):
                fold_mine[t] = folded[:, t * 128 : (t + 1) * 128]
            pool_copy = pltpu.make_async_remote_copy(
                src_ref=fold_mine,
                dst_ref=fold_other,
                send_sem=send_d.at[0],
                recv_sem=recv_d.at[0],
                device_id={"pool": 1 - pool},
                device_id_type=MESH,
            )
            pool_copy.start()
            lane = lax.broadcasted_iota(jnp.int32, (1, 128), 1)
            row = jnp.zeros((1, 128), F32)
            for k in range(8):
                one = jnp.sum(sums[k], keepdims=True) + jnp.sum(sums_g[k], keepdims=True)
                row = jnp.where(lane == k, one, row)
            row_out[...] = row
            row_in[me] = row

        @pl.loop(0, W - 1)
        def _(k):
            peer = peer_at(k)
            pltpu.make_async_remote_copy(
                src_ref=out_r.at[n, :, peer],
                dst_ref=in_r.at[n, :, me],
                send_sem=send_r.at[n],
                recv_sem=recv_r.at[n],
                device_id={"pw": peer},
                device_id_type=MESH,
            ).start()
            if n == 1:
                pltpu.make_async_remote_copy(
                    src_ref=row_out,
                    dst_ref=row_in.at[me],
                    send_sem=send_r.at[2],
                    recv_sem=recv_r.at[2],
                    device_id={"pw": peer},
                    device_id_type=MESH,
                ).start()

        pltpu.make_async_copy(out_r.at[n, :, me], in_r.at[n, :, me], load_sem.at[10 + n]).start()

    pool_copy.wait()
    for t in range(5):
        fold_sum[t] = fold_mine[t] + fold_other[t]
    whole = exact_left(unfold[...], jnp.concatenate([fold_sum[t] for t in range(5)], axis=1))
    for t in range(5):
        spread_out_rows[pl.ds(t * G, G), :] = whole[:, t * 128 : (t + 1) * 128]

    opposite = (W - me) % W
    alone = opposite == me

    def mirror_first():
        return pltpu.make_async_remote_copy(
            src_ref=fold_sum.at[pl.ds(0, 2)],
            dst_ref=fold_mirror.at[pl.ds(0, 2)],
            send_sem=send_d.at[2],
            recv_sem=recv_d.at[2],
            device_id={"pw": opposite},
            device_id_type=MESH,
        )

    mirror_rest = pltpu.make_async_remote_copy(
        src_ref=fold_sum.at[pl.ds(2, 3)],
        dst_ref=fold_mirror.at[pl.ds(2, 3)],
        send_sem=send_d.at[3],
        recv_sem=recv_d.at[3],
        device_id={"pw": W - 1 - me},
        device_id_type=MESH,
    )
    mirror_rest.start()

    @pl.when(jnp.logical_not(alone))
    def _():
        mirror_first().start()

    @pl.when(alone)
    def _():
        for t in range(2):
            fold_mirror[t] = fold_sum[t]

    @pl.loop(0, W - 1)
    def _(k):
        peer = peer_at(k)
        pltpu.make_async_remote_copy(
            src_ref=spread_out.at[:, peer],
            dst_ref=spread_in.at[:, me],
            send_sem=send_d.at[1],
            recv_sem=recv_d.at[1],
            device_id={"pw": peer},
            device_id_type=MESH,
        ).start()

    pltpu.make_async_copy(spread_out.at[:, me], spread_in.at[:, me], load_sem.at[12]).start()

    landed = row_in.at[pl.ds(0, W - 1)]
    pltpu.make_async_copy(landed, landed, recv_r.at[2]).wait()
    lane = lax.broadcasted_iota(jnp.int32, (1, 128), 1)
    totals = jnp.sum(row_in_rows[...], axis=0, keepdims=True) * (1.0 / float(G**3))
    inter = [
        jnp.sum(jnp.where(lane == k, totals, 0.0), axis=1, keepdims=True) for k in range(8)
    ]

    for n in range(2):
        landed = in_r.at[n, :, pl.ds(0, W - 1)]
        pltpu.make_async_copy(landed, landed, recv_r.at[n]).wait()
        pltpu.make_async_copy(out_r.at[n, :, me], in_r.at[n, :, me], load_sem.at[10 + n]).wait()

        @pl.loop(0, R)
        def _(i):
            parts = tiles_at(in_r_rows, (n * BLOCKS + i * 9) * W)
            app = spin(table_left(il_h[...], il_l[...], parts), -1.0)
            kinetic = kinetic_plane(R * me + i)
            shifted = kinetic - energies[0, n]
            scale = 1.0 / (1.0 + kinetic)
            real = jnp.concatenate((app[0], app[2][:, :64]), axis=1)
            imag = jnp.concatenate((app[1], swap64(app[2])[:, :64]), axis=1)
            resp_real, resp_imag = raw[2 * n + 1, 0, i], raw[2 * n + 1, 1, i]
            real = real + shifted * resp_real
            imag = imag + shifted * resp_imag
            for m in range(2):
                orb_real, orb_imag = raw[2 * m, 0, i], raw[2 * m, 1, i]
                over_real, over_imag = inter[(m * 2 + n) * 2], inter[(m * 2 + n) * 2 + 1]
                real = real - (over_real * orb_real - over_imag * orb_imag)
                imag = imag - (over_imag * orb_real + over_real * orb_imag)
            new_buf[n, 0, i] = resp_real - real * scale
            new_buf[n, 1, i] = resp_imag - imag * scale

        pltpu.make_async_copy(new_buf.at[n], new_hbm.at[0, n], store_sem.at[n]).start()

    landed = spread_in.at[:, pl.ds(0, W - 1)]
    pltpu.make_async_copy(landed, landed, recv_d.at[1]).wait()
    pltpu.make_async_copy(spread_out.at[:, me], spread_in.at[:, me], load_sem.at[12]).wait()
    mirror_rest.wait()

    @pl.when(jnp.logical_not(alone))
    def _():
        mirror_first().wait()

    ends = fold_sum[4] + swap64(fold_mirror[4])
    local = (
        (fold_sum[0] + fold_mirror[0], fold_sum[1] + fold_mirror[1]),
        (fold_sum[2] + fold_mirror[3], ends),
        (fold_sum[3] + fold_mirror[2], swap64(ends)),
    )
    for i in range(R):

        def arrived(t):
            return spread_in_rows[pl.ds((t * R + i) * W, W), :]

        top = jnp.concatenate((arrived(0), arrived(2), arrived(3)), axis=0)
        pair = arrived(4)
        end = jnp.concatenate((arrived(1), pair, swap64(pair)), axis=0)
        total = exact_left(merge[...], jnp.concatenate((top, end), axis=1)) + exact_left(
            expand[...], jnp.concatenate(local[i], axis=1)
        )
        dens_buf[i] = total[:, :G] * 0.125
    dens_out = pltpu.make_async_copy(dens_buf, dens_hbm, store_sem.at[2])
    dens_out.start()

    for u in range(4):
        left = out_a.at[u, :, pl.ds(0, W - 1)]
        pltpu.make_async_copy(left, left, send_a.at[u]).wait()
    for n in range(2):
        left = out_r.at[n, :, pl.ds(0, W - 1)]
        pltpu.make_async_copy(left, left, send_r.at[n]).wait()
    left = row_in.at[pl.ds(0, W - 1)]
    pltpu.make_async_copy(left, left, send_r.at[2]).wait()
    left = spread_out.at[:, pl.ds(0, W - 1)]
    pltpu.make_async_copy(left, left, send_d.at[1]).wait()
    for n in range(2):
        pltpu.make_async_copy(new_buf.at[n], new_hbm.at[0, n], store_sem.at[n]).wait()
    dens_out.wait()


def body(orbitals, responses, energies, weights, potential, perturbation):
    held = [jnp.asarray(table) for table in tables()]
    anywhere = pl.BlockSpec(memory_space=pl.ANY)
    scalar = pl.BlockSpec(memory_space=pltpu.SMEM)
    vmem, dma = pltpu.VMEM, pltpu.SemaphoreType.DMA
    return pl.pallas_call(
        kernel,
        out_shape=(
            jax.ShapeDtypeStruct((1, 2, 2, R, G, G), F32),
            jax.ShapeDtypeStruct((R, G, G), F32),
        ),
        in_specs=[anywhere] * 4 + [scalar] * 2 + [anywhere] * len(held),
        out_specs=(anywhere, anywhere),
        scratch_shapes=[vmem(table.shape, BF16) for table in held]
        + [
            vmem((4, 2, R, G, G), F32),
            vmem((R, G, G), F32),
            vmem((R, G, G), F32),
            vmem((4, BLOCKS, W, 1, 128), F32),
            vmem((4, BLOCKS, W, 1, 128), F32),
            vmem((2, BLOCKS, W, 1, 128), F32),
            vmem((2, BLOCKS, W, 1, 128), F32),
            vmem((R, 3, G, 128), F32),
            vmem((R, 3, G, 128), F32),
            vmem((R, G, 256), F32),
            vmem((5, H, 128), F32),
            vmem((5, H, 128), F32),
            vmem((5, H, 128), F32),
            vmem((5, H, 128), F32),
            vmem((15, W, 1, 128), F32),
            vmem((15, W, 1, 128), F32),
            vmem((8, 8, 128), F32),
            vmem((8, 8, G), F32),
            vmem((1, 128), F32),
            vmem((W, 1, 128), F32),
            vmem((2, 2, R, G, G), F32),
            vmem((R, G, G), F32),
            dma((13,)),
            dma((14,)),
            dma((4,)),
            dma((4,)),
            dma((3,)),
            dma((3,)),
            dma((4,)),
            dma((4,)),
            dma((3,)),
        ],
        compiler_params=pltpu.CompilerParams(
            collective_id=0, has_side_effects=True, vmem_limit_bytes=52 * 2**20
        ),
    )(
        orbitals,
        responses,
        jnp.transpose(potential, (1, 0, 2)),
        jnp.transpose(perturbation, (1, 0, 2)),
        energies,
        weights,
        *held,
    )


def solution(mesh):
    placed = (
        P("pool", None, None, "pw", None, None),
        P("pool", None, None, "pw", None, None),
        P("pool", None),
        P("pool"),
        P(None, "pw", None),
        P(None, "pw", None),
    )
    return jax.shard_map(
        body,
        mesh=mesh,
        in_specs=placed,
        out_specs=(P("pool", None, None, "pw", None, None), P("pw", None, None)),
        check_vma=False,
    )
```

```python
import functools
import math

import jax
import jax.numpy as jnp
import ml_dtypes
import numpy as np
from jax import lax
from jax.experimental import pallas as pl
from jax.experimental.pallas import tpu as pltpu
from jax.sharding import PartitionSpec as P

RECIPROCAL_SQUARE = 0.023428
G = 192
W = 64
R = 3
H = 104
BLOCKS = 27
MESH = pl.DeviceIdType.MESH
F32 = jnp.float32
BF16 = jnp.bfloat16


def halves(table):
    high = table.astype(ml_dtypes.bfloat16)
    low = (table - high.astype(np.float64)).astype(ml_dtypes.bfloat16)
    return [high, low]


def tables():
    index = np.arange(G)
    angles = (np.outer(index, index) % G) * (2.0 * math.pi / G)
    cosine = np.cos(angles) / math.sqrt(G)
    sine = np.sin(angles) / math.sqrt(G)
    spread = np.array([R * (s % W) + s // W for s in range(G)])

    def packed(left, right):
        return np.concatenate(
            (left[:, :128], right[:, :128], left[:, 128:], right[:, 128:]), axis=1
        )

    out_left = np.concatenate((cosine[spread], sine[spread]), axis=0)
    in_left = np.concatenate((cosine[:, spread], sine[:, spread]), axis=0)
    right_real = packed(cosine, sine)
    right_imag = packed(-sine, cosine)
    back_real = packed(cosine, -sine)
    back_imag = packed(sine, cosine)
    back = np.concatenate(
        (back_real[:128], back_imag[:128], back_real[128:], back_imag[128:]), axis=0
    )
    fold = np.zeros((H, G))
    unfold = np.zeros((G, H))
    merge = np.zeros((G, G))
    expand = np.zeros((G, H))
    for a in range(H):
        fold[a, a] += 1.0
        fold[a, -a % G] += 1.0
    for s in range(G):
        a = spread[s]
        unfold[s, min(a, G - a)] = 1.0
        merge[a, s] += 1.0
        merge[-a % G, s] += 1.0
        expand[s, min(s, G - s)] = 1.0
    held = []
    for table in (right_real, right_imag, out_left, in_left, back):
        held += halves(table)
    return held + [m.astype(ml_dtypes.bfloat16) for m in (fold, unfold, merge, expand)]


def split(values):
    high = values.astype(BF16)
    return high, (values - high.astype(F32)).astype(BF16)


def dot(left, right):
    return jnp.dot(left, right, preferred_element_type=F32)


def table_left(high, low, values):
    top, rest = split(values)
    return dot(high, top) + (dot(high, rest) + dot(low, top))


def table_right(values, high, low):
    top, rest = split(values)
    return dot(top, high) + (dot(rest, high) + dot(top, low))


def exact_left(table, values):
    top, rest = split(values)
    last = (values - top.astype(F32) - rest.astype(F32)).astype(BF16)
    return dot(table, top) + (dot(table, rest) + dot(table, last))


def swap64(values):
    return pltpu.roll(values, 64, axis=1)


def lane_sign():
    return jnp.where(lax.broadcasted_iota(jnp.int32, (1, 128), 1) < 64, -1.0, 1.0).astype(F32)


def spin(product, sign):
    cos_part, sin_part = product[:G], product[G:]
    return (
        cos_part[:, :128] - sign * sin_part[:, 128:256],
        cos_part[:, 128:256] + sign * sin_part[:, :128],
        cos_part[:, 256:] + (sign * lane_sign()) * swap64(sin_part[:, 256:]),
    )


def rows_of(start, count):
    if isinstance(start, int):
        return pl.ds(start, count)
    return pl.ds(pl.multiple_of(start, 8), count)


def tiles_at(view, start):
    return jnp.concatenate([view[rows_of(start + t * G, G), :] for t in range(3)], axis=1)


def row_sums(values):
    total = values[0:8]
    for s in range(8, G, 8):
        total = total + values[s : s + 8]
    return total


def squared_freq(index):
    freq = jnp.where(index < G // 2, index, index - G).astype(F32)
    return freq * freq


def kinetic_plane(row):
    plane = squared_freq(lax.broadcasted_iota(jnp.int32, (G, G), 0))
    plane = plane + squared_freq(lax.broadcasted_iota(jnp.int32, (G, G), 1))
    return (0.5 * RECIPROCAL_SQUARE) * (squared_freq(row) + plane)


def kernel(
    orb_hbm, resp_hbm, pot_hbm, pert_hbm, energies, weights, *refs
):
    table_hbm = refs[:14]
    new_out, dens_out = refs[14:16]
    tables_in = refs[16:30]
    (
        raw, pot, pert, out_a, in_a, out_r, in_r, orb_space, app_space, dens,
        fold_mine, fold_other, fold_sum, fold_mirror, spread_out, spread_in,
        sums, sums_g, row_out, row_in,
        load_sem, table_sem, send_a, recv_a, send_r, recv_r, send_d, recv_d,
    ) = refs[30:]
    (wr_h, wr_l, wi_h, wi_l, ol_h, ol_l, il_h, il_l, bk_h, bk_l, fold, unfold, merge, expand) = tables_in

    me = lax.axis_index("pw")
    pool = lax.axis_index("pool")

    def load_table(k):
        return pltpu.make_async_copy(table_hbm[k], tables_in[k], table_sem.at[k])

    def load_unit(u):
        source = orb_hbm if u % 2 == 0 else resp_hbm
        return pltpu.make_async_copy(source.at[0, u // 2], raw.at[u], load_sem.at[u])

    loads_pot = pltpu.make_async_copy(pot_hbm, pot, load_sem.at[4])
    loads_pert = pltpu.make_async_copy(pert_hbm, pert, load_sem.at[5])
    for k in range(4):
        load_table(k).start()
    load_unit(0).start()
    for k in range(4, 6):
        load_table(k).start()
    for u in range(1, 4):
        load_unit(u).start()
    for k in range(6, 14):
        load_table(k).start()
    loads_pot.start()
    loads_pert.start()

    barrier = pltpu.get_barrier_semaphore()

    def peer_at(k):
        return me ^ (1 + (k * 37 + 11) % (W - 1))

    @pl.loop(0, W - 1, unroll=9)
    def _(k):
        pl.semaphore_signal(barrier, inc=1, device_id={"pw": peer_at(k)}, device_id_type=MESH)

    pl.semaphore_signal(barrier, inc=1, device_id={"pool": 1 - pool}, device_id_type=MESH)

    out_a_rows = out_a.reshape(4 * BLOCKS * W, 128)
    in_a_rows = in_a.reshape(4 * BLOCKS * W, 128)
    out_r_rows = out_r.reshape(2 * BLOCKS * W, 128)
    in_r_rows = in_r.reshape(2 * BLOCKS * W, 128)
    spread_out_rows = spread_out.reshape(15 * W, 128)
    spread_in_rows = spread_in.reshape(15 * W, 128)
    row_in_rows = row_in.reshape(W, 128)

    for k in range(6):
        load_table(k).wait()

    def piece_a(ref, u, part, who):
        if u == 0:
            return ref.at[u, :, part, who]
        if u == 1:
            return ref.at[u, :, :, who]
        return ref.at[u, pl.ds(3 * part, 3), :, who]

    def send_piece_a(u, part, peer):
        pltpu.make_async_remote_copy(
            src_ref=piece_a(out_a, u, part, peer),
            dst_ref=piece_a(in_a, u, part, me),
            send_sem=send_a.at[u, part],
            recv_sem=recv_a.at[u, part],
            device_id={"pw": peer},
            device_id_type=MESH,
        ).start()

    def wait_bytes(ref, sem):
        pltpu.make_async_copy(ref, ref, sem).wait()

    others = pl.ds(0, W - 1)

    def own_a(u):
        return pltpu.make_async_copy(
            out_a.at[u, :, :, me], in_a.at[u, :, :, me], load_sem.at[6 + u]
        )

    def plane(u, i):
        planes = table_right(raw[u, 0, i], wr_h[...], wr_l[...]) + table_right(
            raw[u, 1, i], wi_h[...], wi_l[...]
        )
        parts = spin(table_left(ol_h[...], ol_l[...], planes), 1.0)
        for j in range(R):
            for t in range(3):
                start = (u * BLOCKS + (j * 3 + t) * R + i) * W
                out_a_rows[rows_of(start, W), :] = parts[t][j * W : (j + 1) * W]

    load_unit(0).wait()
    for i in range(R):
        plane(0, i)
        if i == 0:
            pl.semaphore_wait(barrier, W)

        @pl.loop(0, W - 1, unroll=9)
        def _(k):
            send_piece_a(0, i, peer_at(k))

    own_a(0).start()
    for u in range(1, 4):
        load_unit(u).wait()

        @pl.loop(0, R)
        def _(i):
            plane(u, i)

        if u == 1:

            @pl.loop(0, W - 1, unroll=9)
            def _(k):
                send_piece_a(1, 0, peer_at(k))

        own_a(u).start()

    for j in range(R):

        @pl.loop(0, W - 1, unroll=9)
        def _(k):
            peer = peer_at(k)
            send_piece_a(2, j, peer)
            send_piece_a(3, j, peer)

    for k in range(6, 14):
        load_table(k).wait()

    sums_g[...] = jnp.zeros_like(sums_g)

    @pl.loop(0, R)
    def _(i):
        kinetic = kinetic_plane(R * me + i)
        for n in range(2):
            shifted = kinetic - energies[0, n]
            real = shifted * raw[2 * n + 1, 0, i]
            imag = shifted * raw[2 * n + 1, 1, i]
            for m in range(2):
                left_real, left_imag = raw[2 * m, 0, i], raw[2 * m, 1, i]
                at = (m * 2 + n) * 2
                sums_g[at] += row_sums(left_real * real + left_imag * imag)
                sums_g[at + 1] += row_sums(left_real * imag - left_imag * real)

    loads_pot.wait()
    loads_pert.wait()
    sums[...] = jnp.zeros_like(sums)

    def columns(n, j):
        at = j * 3 * G
        first = 2 * n * BLOCKS * W
        second = (2 * n + 1) * BLOCKS * W
        orb = spin(table_left(il_h[...], il_l[...], tiles_at(in_a_rows, first + at)), 1.0)
        resp = spin(table_left(il_h[...], il_l[...], tiles_at(in_a_rows, second + at)), 1.0)
        pot_top = pot[j, :, 0:128]
        pert_top = pert[j, :, 0:128]
        pot_end = jnp.concatenate((pot[j, :, 128:G], pot[j, :, 128:G]), axis=1)
        pert_end = jnp.concatenate((pert[j, :, 128:G], pert[j, :, 128:G]), axis=1)
        app = (
            pot_top * resp[0] + pert_top * orb[0],
            pot_top * resp[1] + pert_top * orb[1],
            pot_end * resp[2] + pert_end * orb[2],
        )
        ends = orb[2] * resp[2]
        density = (2.0 * weights[0]) * jnp.concatenate(
            (orb[0] * resp[0] + orb[1] * resp[1], ends + swap64(ends)), axis=1
        )

        def overlap(left, right, slot):
            sums[slot] += row_sums(left[0] * right[0] + left[1] * right[1] + left[2] * right[2])
            sums[slot + 1] += row_sums(
                left[0] * right[1]
                - left[1] * right[0]
                - lane_sign() * left[2] * swap64(right[2])
            )

        if n == 0:
            overlap(orb, app, 0)
            dens[j] = density
            for t in range(3):
                orb_space[j, t] = orb[t]
                app_space[j, t] = app[t]
        else:
            dens[j] = dens[j] + density
            orb_first = [orb_space[j, t] for t in range(3)]
            app_first = [app_space[j, t] for t in range(3)]
            overlap(orb_first, app, 2)
            overlap(orb, app_first, 4)
            overlap(orb, app, 6)
        product = table_left(ol_h[...], ol_l[...], jnp.concatenate(app, axis=1))
        turned = jnp.concatenate(spin(product, -1.0), axis=1)
        back = table_right(turned, bk_h[...], bk_l[...])
        for i in range(R):
            for t in range(3):
                start = (n * BLOCKS + (i * 3 + t) * R + j) * W
                out_r_rows[rows_of(start, W), :] = back[
                    i * W : (i + 1) * W, t * 128 : (t + 1) * 128
                ]

    def piece_r(ref, n, part, who):
        if n == 0:
            return ref.at[n, :, :, who]
        return ref.at[n, :, part, who]

    def send_piece_r(n, part, peer):
        pltpu.make_async_remote_copy(
            src_ref=piece_r(out_r, n, part, peer),
            dst_ref=piece_r(in_r, n, part, me),
            send_sem=send_r.at[n, part],
            recv_sem=recv_r.at[n, part],
            device_id={"pw": peer},
            device_id_type=MESH,
        ).start()

    def own_r(n):
        return pltpu.make_async_copy(
            out_r.at[n, :, :, me], in_r.at[n, :, :, me], load_sem.at[10 + n]
        )

    for i in range(R):
        wait_bytes(piece_a(in_a, 0, i, others), recv_a.at[0, i])
    wait_bytes(piece_a(in_a, 1, 0, others), recv_a.at[1, 0])
    own_a(0).wait()
    own_a(1).wait()

    @pl.loop(0, R)
    def _(j):
        columns(0, j)

    @pl.loop(0, W - 1, unroll=9)
    def _(k):
        send_piece_r(0, 0, peer_at(k))

    own_r(0).start()
    own_a(2).wait()
    own_a(3).wait()

    strips_of = ((0, 2), (2, 1), (3, 2))

    def pool_copy(j):
        strips = pl.ds(*strips_of[j])
        return pltpu.make_async_remote_copy(
            src_ref=fold_mine.at[strips],
            dst_ref=fold_other.at[strips],
            send_sem=send_d.at[j],
            recv_sem=recv_d.at[j],
            device_id={"pool": 1 - pool},
            device_id_type=MESH,
        )

    lane = lax.broadcasted_iota(jnp.int32, (1, 128), 1)
    for j in range(R):
        for u in (2, 3):
            wait_bytes(piece_a(in_a, u, j, others), recv_a.at[u, j])
        columns(1, j)
        if j == 0:
            strips = (dens[0, :, 0:128], dens[0, :, 128:256])
        elif j == 1:
            strips = (dens[1, :, 0:128],)
        else:
            strips = (
                dens[2, :, 0:128],
                jnp.where(lane < 64, dens[1, :, 128:256], dens[2, :, 128:256]),
            )
        first, count = strips_of[j]
        folded = exact_left(fold[...], jnp.concatenate(strips, axis=1))
        for t in range(count):
            fold_mine[first + t] = folded[:, t * 128 : (t + 1) * 128]
        pool_copy(j).start()

        @pl.loop(0, W - 1, unroll=9)
        def _(k):
            send_piece_r(1, j, peer_at(k))

    own_r(1).start()
    row = jnp.zeros((1, 128), F32)
    for k in range(8):
        one = jnp.sum(sums[k], keepdims=True) + jnp.sum(sums_g[k], keepdims=True)
        row = jnp.where(lane == k, one, row)
    row_out[...] = row
    row_in[me] = row

    @pl.loop(0, W - 1, unroll=9)
    def _(k):
        pltpu.make_async_remote_copy(
            src_ref=row_out,
            dst_ref=row_in.at[me],
            send_sem=send_r.at[2, 0],
            recv_sem=recv_r.at[2, 0],
            device_id={"pw": peer_at(k)},
            device_id_type=MESH,
        ).start()

    for j in range(R):
        pool_copy(j).wait()
    for t in range(5):
        fold_sum[t] = fold_mine[t] + fold_other[t]
    whole = exact_left(unfold[...], jnp.concatenate([fold_sum[t] for t in range(5)], axis=1))
    for t in range(5):
        spread_out_rows[pl.ds(t * G, G), :] = whole[:, t * 128 : (t + 1) * 128]

    opposite = (W - me) % W
    alone = opposite == me

    def mirror_first():
        return pltpu.make_async_remote_copy(
            src_ref=fold_sum.at[pl.ds(0, 2)],
            dst_ref=fold_mirror.at[pl.ds(0, 2)],
            send_sem=send_d.at[3],
            recv_sem=recv_d.at[3],
            device_id={"pw": opposite},
            device_id_type=MESH,
        )

    mirror_rest = pltpu.make_async_remote_copy(
        src_ref=fold_sum.at[pl.ds(2, 3)],
        dst_ref=fold_mirror.at[pl.ds(2, 3)],
        send_sem=send_d.at[4],
        recv_sem=recv_d.at[4],
        device_id={"pw": W - 1 - me},
        device_id_type=MESH,
    )
    mirror_rest.start()

    @pl.when(jnp.logical_not(alone))
    def _():
        mirror_first().start()

    @pl.when(alone)
    def _():
        for t in range(2):
            fold_mirror[t] = fold_sum[t]

    @pl.loop(0, W - 1, unroll=9)
    def _(k):
        peer = peer_at(k)
        pltpu.make_async_remote_copy(
            src_ref=spread_out.at[:, peer],
            dst_ref=spread_in.at[:, me],
            send_sem=send_d.at[5],
            recv_sem=recv_d.at[5],
            device_id={"pw": peer},
            device_id_type=MESH,
        ).start()

    pltpu.make_async_copy(spread_out.at[:, me], spread_in.at[:, me], load_sem.at[12]).start()

    wait_bytes(row_in.at[others], recv_r.at[2, 0])
    totals = jnp.sum(row_in_rows[...], axis=0, keepdims=True) * (1.0 / float(G**3))
    inter = [
        jnp.sum(jnp.where(lane == k, totals, 0.0), axis=1, keepdims=True) for k in range(8)
    ]

    def update(n):
        @pl.loop(0, R)
        def _(i):
            parts = tiles_at(in_r_rows, (n * BLOCKS + i * 9) * W)
            app = spin(table_left(il_h[...], il_l[...], parts), -1.0)
            kinetic = kinetic_plane(R * me + i)
            shifted = kinetic - energies[0, n]
            scale = 1.0 / (1.0 + kinetic)
            real = jnp.concatenate((app[0], app[2][:, :64]), axis=1)
            imag = jnp.concatenate((app[1], swap64(app[2])[:, :64]), axis=1)
            resp_real, resp_imag = raw[2 * n + 1, 0, i], raw[2 * n + 1, 1, i]
            real = real + shifted * resp_real
            imag = imag + shifted * resp_imag
            for m in range(2):
                orb_real, orb_imag = raw[2 * m, 0, i], raw[2 * m, 1, i]
                over_real, over_imag = inter[(m * 2 + n) * 2], inter[(m * 2 + n) * 2 + 1]
                real = real - (over_real * orb_real - over_imag * orb_imag)
                imag = imag - (over_imag * orb_real + over_real * orb_imag)
            new_out[0, n, 0, i] = resp_real - real * scale
            new_out[0, n, 1, i] = resp_imag - imag * scale


    wait_bytes(piece_r(in_r, 0, 0, others), recv_r.at[0, 0])
    own_r(0).wait()
    update(0)

    wait_bytes(spread_in.at[:, others], recv_d.at[5])
    pltpu.make_async_copy(spread_out.at[:, me], spread_in.at[:, me], load_sem.at[12]).wait()
    mirror_rest.wait()

    @pl.when(jnp.logical_not(alone))
    def _():
        mirror_first().wait()

    ends = fold_sum[4] + swap64(fold_mirror[4])
    local = (
        (fold_sum[0] + fold_mirror[0], fold_sum[1] + fold_mirror[1]),
        (fold_sum[2] + fold_mirror[3], ends),
        (fold_sum[3] + fold_mirror[2], swap64(ends)),
    )
    for i in range(R):

        def arrived(t):
            return spread_in_rows[pl.ds((t * R + i) * W, W), :]

        top = jnp.concatenate((arrived(0), arrived(2), arrived(3)), axis=0)
        pair = arrived(4)
        end = jnp.concatenate((arrived(1), pair, swap64(pair)), axis=0)
        total = exact_left(merge[...], jnp.concatenate((top, end), axis=1)) + exact_left(
            expand[...], jnp.concatenate(local[i], axis=1)
        )
        dens_out[i] = total[:, :G] * 0.125

    for j in range(R):
        wait_bytes(piece_r(in_r, 1, j, others), recv_r.at[1, j])
    own_r(1).wait()
    update(1)

    for j in range(R):
        for u in (0, 2, 3):
            wait_bytes(piece_a(out_a, u, j, others), send_a.at[u, j])
        wait_bytes(piece_r(out_r, 1, j, others), send_r.at[1, j])
    wait_bytes(piece_a(out_a, 1, 0, others), send_a.at[1, 0])
    wait_bytes(piece_r(out_r, 0, 0, others), send_r.at[0, 0])
    wait_bytes(row_in.at[others], send_r.at[2, 0])
    wait_bytes(spread_out.at[:, others], send_d.at[5])


def in_hbm(array):
    return pltpu.with_memory_space_constraint(array, pltpu.HBM)


def body(orbitals, responses, energies, weights, potential, perturbation):
    held = [in_hbm(jnp.asarray(table)) for table in tables()]
    anywhere = pl.BlockSpec(memory_space=pl.ANY)
    scalar = pl.BlockSpec(memory_space=pltpu.SMEM)
    vmem, dma = pltpu.VMEM, pltpu.SemaphoreType.DMA
    return pl.pallas_call(
        kernel,
        out_shape=(
            pltpu.VMEM((1, 2, 2, R, G, G), F32),
            pltpu.VMEM((R, G, G), F32),
        ),
        in_specs=[anywhere] * 4 + [scalar] * 2 + [anywhere] * len(held),
        out_specs=(pl.BlockSpec(memory_space=pltpu.VMEM),) * 2,
        scratch_shapes=[vmem(table.shape, BF16) for table in held]
        + [
            vmem((4, 2, R, G, G), F32),
            vmem((R, G, G), F32),
            vmem((R, G, G), F32),
            vmem((4, 9, R, W, 1, 128), F32),
            vmem((4, 9, R, W, 1, 128), F32),
            vmem((2, 9, R, W, 1, 128), F32),
            vmem((2, 9, R, W, 1, 128), F32),
            vmem((R, 3, G, 128), F32),
            vmem((R, 3, G, 128), F32),
            vmem((R, G, 256), F32),
            vmem((5, H, 128), F32),
            vmem((5, H, 128), F32),
            vmem((5, H, 128), F32),
            vmem((5, H, 128), F32),
            vmem((15, W, 1, 128), F32),
            vmem((15, W, 1, 128), F32),
            vmem((8, 8, 128), F32),
            vmem((8, 8, G), F32),
            vmem((1, 128), F32),
            vmem((W, 1, 128), F32),
            dma((13,)),
            dma((14,)),
            dma((4, R)),
            dma((4, R)),
            dma((3, R)),
            dma((3, R)),
            dma((6,)),
            dma((6,)),
        ],
        compiler_params=pltpu.CompilerParams(
            collective_id=0, has_side_effects=True, vmem_limit_bytes=56 * 2**20
        ),
    )(
        in_hbm(orbitals),
        in_hbm(responses),
        in_hbm(jnp.transpose(potential, (1, 0, 2))),
        in_hbm(jnp.transpose(perturbation, (1, 0, 2))),
        energies,
        weights,
        *held,
    )


def solution(mesh):
    placed = (
        P("pool", None, None, "pw", None, None),
        P("pool", None, None, "pw", None, None),
        P("pool", None),
        P("pool"),
        P(None, "pw", None),
        P(None, "pw", None),
    )
    return jax.shard_map(
        body,
        mesh=mesh,
        in_specs=placed,
        out_specs=(P("pool", None, None, "pw", None, None), P("pw", None, None)),
        check_vma=False,
    )
```

```python
import functools
import math

import jax
import jax.numpy as jnp
import ml_dtypes
import numpy as np
from jax import lax
from jax.experimental import pallas as pl
from jax.experimental.pallas import tpu as pltpu
from jax.sharding import PartitionSpec as P

RECIPROCAL_SQUARE = 0.023428
G = 192
W = 64
R = 3
H = 104
K = G // 2 + 1
BLOCKS = 27
MESH = pl.DeviceIdType.MESH
F32 = jnp.float32
BF16 = jnp.bfloat16


def halves(table):
    high = table.astype(ml_dtypes.bfloat16)
    low = (table - high.astype(np.float64)).astype(ml_dtypes.bfloat16)
    return [high, low]


def tables():
    index = np.arange(G)
    angles = (np.outer(index, index) % G) * (2.0 * math.pi / G)
    cosine = np.cos(angles) / math.sqrt(G)
    sine = np.sin(angles) / math.sqrt(G)
    spread = np.array([R * (s % W) + s // W for s in range(G)])

    def packed(left, right):
        return np.concatenate(
            (left[:, :128], right[:, :128], left[:, 128:], right[:, 128:]), axis=1
        )

    out_left = np.concatenate((cosine[spread], sine[spread]), axis=0)
    in_left = np.concatenate((cosine[:, spread], sine[:, spread]), axis=0)
    right_real = packed(cosine, sine)
    right_imag = packed(-sine, cosine)
    back_real = packed(cosine, -sine)
    back_imag = packed(sine, cosine)
    back = np.concatenate(
        (back_real[:128], back_imag[:128], back_real[128:], back_imag[128:]), axis=0
    )
    fold = np.zeros((H, G))
    unfold = np.zeros((G, H))
    merge = np.zeros((G, G))
    expand = np.zeros((G, H))
    for a in range(H):
        fold[a, a] += 1.0
        fold[a, -a % G] += 1.0
    for s in range(G):
        a = spread[s]
        unfold[s, min(a, G - a)] = 1.0
        merge[a, s] += 1.0
        merge[-a % G, s] += 1.0
        expand[s, min(s, G - s)] = 1.0
    held = []
    for table in (right_real, right_imag, out_left, in_left, back):
        held += halves(table)
    return held + [m.astype(ml_dtypes.bfloat16) for m in (fold, unfold, merge, expand)]


def split(values):
    high = values.astype(BF16)
    return high, (values - high.astype(F32)).astype(BF16)


def dot(left, right):
    return jnp.dot(left, right, preferred_element_type=F32)


def table_left(high, low, values):
    top, rest = split(values)
    return dot(high, top) + (dot(high, rest) + dot(low, top))


def table_right(values, high, low):
    top, rest = split(values)
    return dot(top, high) + (dot(rest, high) + dot(top, low))


def exact_left(table, values):
    top, rest = split(values)
    last = (values - top.astype(F32) - rest.astype(F32)).astype(BF16)
    return dot(table, top) + (dot(table, rest) + dot(table, last))


def swap64(values):
    return pltpu.roll(values, 64, axis=1)


def lane_sign():
    return jnp.where(lax.broadcasted_iota(jnp.int32, (1, 128), 1) < 64, -1.0, 1.0).astype(F32)


def spin(product, sign):
    cos_part, sin_part = product[:G], product[G:]
    return (
        cos_part[:, :128] - sign * sin_part[:, 128:256],
        cos_part[:, 128:256] + sign * sin_part[:, :128],
        cos_part[:, 256:] + (sign * lane_sign()) * swap64(sin_part[:, 256:]),
    )


def rows_of(start, count):
    if isinstance(start, int):
        return pl.ds(start, count)
    return pl.ds(pl.multiple_of(start, 8), count)


def tiles_at(view, start):
    return jnp.concatenate([view[rows_of(start + t * G, G), :] for t in range(3)], axis=1)


def row_sums(values):
    total = values[0:8]
    for s in range(8, G, 8):
        total = total + values[s : s + 8]
    return total


def squared_freq(index):
    freq = jnp.where(index < G // 2, index, index - G).astype(F32)
    return freq * freq


def kinetic_plane(row):
    plane = squared_freq(lax.broadcasted_iota(jnp.int32, (G, G), 0))
    plane = plane + squared_freq(lax.broadcasted_iota(jnp.int32, (G, G), 1))
    return (0.5 * RECIPROCAL_SQUARE) * (squared_freq(row) + plane)


def kernel(
    orb_hbm, resp_hbm, pot_hbm, pert_hbm, energies, weights, *refs
):
    table_hbm = refs[:14]
    new_out, dens_out = refs[14:16]
    tables_in = refs[16:30]
    (
        raw, pot, pert, out_a, in_a, out_r, in_r, orb_space, app_space, dens,
        fold_mine, fold_other, fold_sum, fold_mirror, spread_out, spread_in,
        sums, sums_g, row_out, row_in,
        load_sem, table_sem, send_a, recv_a, send_r, recv_r, send_d, recv_d,
    ) = refs[30:]
    (wr_h, wr_l, wi_h, wi_l, ol_h, ol_l, il_h, il_l, bk_h, bk_l, fold, unfold, merge, expand) = tables_in

    me = lax.axis_index("pw")
    pool = lax.axis_index("pool")

    def load_table(k):
        return pltpu.make_async_copy(table_hbm[k], tables_in[k], table_sem.at[k])

    def load_unit(u):
        source = orb_hbm if u % 2 == 0 else resp_hbm
        return pltpu.make_async_copy(source.at[0, u // 2], raw.at[u], load_sem.at[u])

    loads_pot = pltpu.make_async_copy(pot_hbm, pot, load_sem.at[4])
    loads_pert = pltpu.make_async_copy(pert_hbm, pert, load_sem.at[5])
    for k in range(4):
        load_table(k).start()
    load_unit(0).start()
    for k in range(4, 6):
        load_table(k).start()
    out_a_rows = out_a.reshape(4 * BLOCKS * W, 128)
    in_a_rows = in_a.reshape(4 * BLOCKS * W, 128)
    out_r_rows = out_r.reshape(2 * BLOCKS * W, 128)
    in_r_rows = in_r.reshape(2 * BLOCKS * W, 128)
    spread_out_rows = spread_out.reshape(15 * W, 128)
    spread_in_rows = spread_in.reshape(15 * W, 128)
    row_in_rows = row_in.reshape(W, 128)
    fold_mine_rows = fold_mine.reshape(5 * H, 128)
    fold_other_rows = fold_other.reshape(5 * H, 128)
    fold_sum_rows = fold_sum.reshape(5 * H, 128)
    fold_mirror_rows = fold_mirror.reshape(5 * H, 128)

    for t in range(5):
        fold_other_rows[pl.ds(t * H + H - 8, 8), :] = jnp.zeros((8, 128), F32)
        fold_mirror_rows[pl.ds(t * H + H - 8, 8), :] = jnp.zeros((8, 128), F32)
    kept = pl.ds(0, K)
    mirrors = ((W - me) % W, W - 1 - me)

    barrier = pltpu.get_barrier_semaphore()

    def peer_at(k):
        return me ^ (1 + (k * 37 + 11) % (W - 1))

    @pl.loop(0, W - 1, unroll=9)
    def _(k):
        pl.semaphore_signal(barrier, inc=1, device_id={"pw": peer_at(k)}, device_id_type=MESH)

    for who in (me, *mirrors):
        pl.semaphore_signal(
            barrier, inc=1, device_id={"pool": 1 - pool, "pw": who}, device_id_type=MESH
        )

    for u in range(1, 4):
        load_unit(u).start()
    for k in range(6, 14):
        load_table(k).start()
    loads_pot.start()
    loads_pert.start()

    for k in range(6):
        load_table(k).wait()

    def piece_a(ref, u, part, who):
        if u == 0:
            return ref.at[u, :, part, who]
        if u == 1:
            return ref.at[u, :, :, who]
        return ref.at[u, pl.ds(3 * part, 3), :, who]

    def send_piece_a(u, part, peer):
        pltpu.make_async_remote_copy(
            src_ref=piece_a(out_a, u, part, peer),
            dst_ref=piece_a(in_a, u, part, me),
            send_sem=send_a.at[u, part],
            recv_sem=recv_a.at[u, part],
            device_id={"pw": peer},
            device_id_type=MESH,
        ).start()

    def wait_bytes(ref, sem):
        pltpu.make_async_copy(ref, ref, sem).wait()

    others = pl.ds(0, W - 1)

    def own_a(u):
        return pltpu.make_async_copy(
            out_a.at[u, :, :, me], in_a.at[u, :, :, me], load_sem.at[6 + u]
        )

    def plane(u, i):
        planes = table_right(raw[u, 0, i], wr_h[...], wr_l[...]) + table_right(
            raw[u, 1, i], wi_h[...], wi_l[...]
        )
        parts = spin(table_left(ol_h[...], ol_l[...], planes), 1.0)
        for j in range(R):
            for t in range(3):
                start = (u * BLOCKS + (j * 3 + t) * R + i) * W
                out_a_rows[rows_of(start, W), :] = parts[t][j * W : (j + 1) * W]

    load_unit(0).wait()
    for i in range(R):
        plane(0, i)
        if i == 0:
            pl.semaphore_wait(barrier, W + 2)

        @pl.loop(0, W - 1, unroll=9)
        def _(k):
            send_piece_a(0, i, peer_at(k))

    own_a(0).start()
    for u in range(1, 4):
        load_unit(u).wait()

        @pl.loop(0, R)
        def _(i):
            plane(u, i)

        if u == 1:

            @pl.loop(0, W - 1, unroll=9)
            def _(k):
                send_piece_a(1, 0, peer_at(k))

        own_a(u).start()

    for j in range(R):

        @pl.loop(0, W - 1, unroll=9)
        def _(k):
            peer = peer_at(k)
            send_piece_a(2, j, peer)
            send_piece_a(3, j, peer)

    for k in range(6, 14):
        load_table(k).wait()

    sums_g[...] = jnp.zeros_like(sums_g)

    @pl.loop(0, R)
    def _(i):
        kinetic = kinetic_plane(R * me + i)
        for n in range(2):
            shifted = kinetic - energies[0, n]
            real = shifted * raw[2 * n + 1, 0, i]
            imag = shifted * raw[2 * n + 1, 1, i]
            for m in range(2):
                left_real, left_imag = raw[2 * m, 0, i], raw[2 * m, 1, i]
                at = (m * 2 + n) * 2
                sums_g[at] += row_sums(left_real * real + left_imag * imag)
                sums_g[at + 1] += row_sums(left_real * imag - left_imag * real)

    loads_pot.wait()
    loads_pert.wait()
    sums[...] = jnp.zeros_like(sums)

    def columns(n, j):
        at = j * 3 * G
        first = 2 * n * BLOCKS * W
        second = (2 * n + 1) * BLOCKS * W
        orb = spin(table_left(il_h[...], il_l[...], tiles_at(in_a_rows, first + at)), 1.0)
        resp = spin(table_left(il_h[...], il_l[...], tiles_at(in_a_rows, second + at)), 1.0)
        pot_top = pot[j, :, 0:128]
        pert_top = pert[j, :, 0:128]
        pot_end = jnp.concatenate((pot[j, :, 128:G], pot[j, :, 128:G]), axis=1)
        pert_end = jnp.concatenate((pert[j, :, 128:G], pert[j, :, 128:G]), axis=1)
        app = (
            pot_top * resp[0] + pert_top * orb[0],
            pot_top * resp[1] + pert_top * orb[1],
            pot_end * resp[2] + pert_end * orb[2],
        )
        ends = orb[2] * resp[2]
        density = (2.0 * weights[0]) * jnp.concatenate(
            (orb[0] * resp[0] + orb[1] * resp[1], ends + swap64(ends)), axis=1
        )

        def overlap(left, right, slot):
            sums[slot] += row_sums(left[0] * right[0] + left[1] * right[1] + left[2] * right[2])
            sums[slot + 1] += row_sums(
                left[0] * right[1]
                - left[1] * right[0]
                - lane_sign() * left[2] * swap64(right[2])
            )

        if n == 0:
            overlap(orb, app, 0)
            dens[j] = density
            for t in range(3):
                orb_space[j, t] = orb[t]
                app_space[j, t] = app[t]
        else:
            dens[j] = dens[j] + density
            orb_first = [orb_space[j, t] for t in range(3)]
            app_first = [app_space[j, t] for t in range(3)]
            overlap(orb_first, app, 2)
            overlap(orb, app_first, 4)
            overlap(orb, app, 6)
        product = table_left(ol_h[...], ol_l[...], jnp.concatenate(app, axis=1))
        turned = jnp.concatenate(spin(product, -1.0), axis=1)
        back = table_right(turned, bk_h[...], bk_l[...])
        for i in range(R):
            for t in range(3):
                start = (n * BLOCKS + (i * 3 + t) * R + j) * W
                out_r_rows[rows_of(start, W), :] = back[
                    i * W : (i + 1) * W, t * 128 : (t + 1) * 128
                ]

    def piece_r(ref, n, part, who):
        if n == 0:
            return ref.at[n, :, :, who]
        return ref.at[n, :, part, who]

    def send_piece_r(n, part, peer):
        pltpu.make_async_remote_copy(
            src_ref=piece_r(out_r, n, part, peer),
            dst_ref=piece_r(in_r, n, part, me),
            send_sem=send_r.at[n, part],
            recv_sem=recv_r.at[n, part],
            device_id={"pw": peer},
            device_id_type=MESH,
        ).start()

    def own_r(n):
        return pltpu.make_async_copy(
            out_r.at[n, :, :, me], in_r.at[n, :, :, me], load_sem.at[10 + n]
        )

    for i in range(R):
        wait_bytes(piece_a(in_a, 0, i, others), recv_a.at[0, i])
    wait_bytes(piece_a(in_a, 1, 0, others), recv_a.at[1, 0])
    own_a(0).wait()
    own_a(1).wait()

    @pl.loop(0, R)
    def _(j):
        columns(0, j)

    @pl.loop(0, W - 1, unroll=9)
    def _(k):
        send_piece_r(0, 0, peer_at(k))

    own_r(0).start()
    own_a(2).wait()
    own_a(3).wait()

    strips_of = ((0, 2), (2, 1), (3, 2))

    def pool_copy(j):
        strips = pl.ds(*strips_of[j])
        return pltpu.make_async_remote_copy(
            src_ref=fold_mine.at[strips, kept],
            dst_ref=fold_other.at[strips, kept],
            send_sem=send_d.at[j],
            recv_sem=recv_d.at[j],
            device_id={"pool": 1 - pool},
            device_id_type=MESH,
        )

    lane = lax.broadcasted_iota(jnp.int32, (1, 128), 1)
    for j in range(R):
        for u in (2, 3):
            wait_bytes(piece_a(in_a, u, j, others), recv_a.at[u, j])
        columns(1, j)
        if j == 0:
            strips = (dens[0, :, 0:128], dens[0, :, 128:256])
        elif j == 1:
            strips = (dens[1, :, 0:128],)
        else:
            strips = (
                dens[2, :, 0:128],
                jnp.where(lane < 64, dens[1, :, 128:256], dens[2, :, 128:256]),
            )
        first, count = strips_of[j]
        folded = exact_left(fold[...], jnp.concatenate(strips, axis=1))
        for t in range(count):
            fold_mine_rows[pl.ds((first + t) * H, H), :] = folded[:, t * 128 : (t + 1) * 128]
        pool_copy(j).start()

        @pl.loop(0, W - 1, unroll=9)
        def _(k):
            send_piece_r(1, j, peer_at(k))

    own_r(1).start()
    row = jnp.zeros((1, 128), F32)
    for k in range(8):
        one = jnp.sum(sums[k], keepdims=True) + jnp.sum(sums_g[k], keepdims=True)
        row = jnp.where(lane == k, one, row)
    row_out[...] = row
    row_in[me] = row

    @pl.loop(0, W - 1, unroll=9)
    def _(k):
        pltpu.make_async_remote_copy(
            src_ref=row_out,
            dst_ref=row_in.at[me],
            send_sem=send_r.at[2, 0],
            recv_sem=recv_r.at[2, 0],
            device_id={"pw": peer_at(k)},
            device_id_type=MESH,
        ).start()

    for j in range(R):
        pool_copy(j).wait()
    summed = [
        fold_mine_rows[pl.ds(t * H, H), :] + fold_other_rows[pl.ds(t * H, H), :] for t in range(5)
    ]
    for t in range(5):
        fold_sum_rows[pl.ds(t * H, H), :] = summed[t]
    whole = exact_left(unfold[...], jnp.concatenate(summed, axis=1))
    for t in range(5):
        spread_out_rows[pl.ds(t * G, G), :] = whole[:, t * 128 : (t + 1) * 128]

    def mirror_copy(part):
        strips = (pl.ds(0, 2), pl.ds(2, 3))[part]
        return pltpu.make_async_remote_copy(
            src_ref=fold_sum.at[strips, kept],
            dst_ref=fold_mirror.at[strips, kept],
            send_sem=send_d.at[3 + part],
            recv_sem=recv_d.at[3 + part],
            device_id={"pool": 1 - pool, "pw": mirrors[part]},
            device_id_type=MESH,
        )

    for part in range(2):
        mirror_copy(part).start()

    @pl.loop(0, W - 1, unroll=9)
    def _(k):
        peer = peer_at(k)
        pltpu.make_async_remote_copy(
            src_ref=spread_out.at[:, peer],
            dst_ref=spread_in.at[:, me],
            send_sem=send_d.at[5],
            recv_sem=recv_d.at[5],
            device_id={"pw": peer},
            device_id_type=MESH,
        ).start()

    pltpu.make_async_copy(spread_out.at[:, me], spread_in.at[:, me], load_sem.at[12]).start()

    wait_bytes(row_in.at[others], recv_r.at[2, 0])
    totals = jnp.sum(row_in_rows[...], axis=0, keepdims=True) * (1.0 / float(G**3))
    inter = [
        jnp.sum(jnp.where(lane == k, totals, 0.0), axis=1, keepdims=True) for k in range(8)
    ]

    def update(n):
        @pl.loop(0, R)
        def _(i):
            parts = tiles_at(in_r_rows, (n * BLOCKS + i * 9) * W)
            app = spin(table_left(il_h[...], il_l[...], parts), -1.0)
            kinetic = kinetic_plane(R * me + i)
            shifted = kinetic - energies[0, n]
            scale = 1.0 / (1.0 + kinetic)
            real = jnp.concatenate((app[0], app[2][:, :64]), axis=1)
            imag = jnp.concatenate((app[1], swap64(app[2])[:, :64]), axis=1)
            resp_real, resp_imag = raw[2 * n + 1, 0, i], raw[2 * n + 1, 1, i]
            real = real + shifted * resp_real
            imag = imag + shifted * resp_imag
            for m in range(2):
                orb_real, orb_imag = raw[2 * m, 0, i], raw[2 * m, 1, i]
                over_real, over_imag = inter[(m * 2 + n) * 2], inter[(m * 2 + n) * 2 + 1]
                real = real - (over_real * orb_real - over_imag * orb_imag)
                imag = imag - (over_imag * orb_real + over_real * orb_imag)
            new_out[0, n, 0, i] = resp_real - real * scale
            new_out[0, n, 1, i] = resp_imag - imag * scale


    wait_bytes(piece_r(in_r, 0, 0, others), recv_r.at[0, 0])
    own_r(0).wait()
    update(0)

    for j in range(R):
        wait_bytes(piece_r(in_r, 1, j, others), recv_r.at[1, j])
    own_r(1).wait()
    update(1)

    wait_bytes(spread_in.at[:, others], recv_d.at[5])
    pltpu.make_async_copy(spread_out.at[:, me], spread_in.at[:, me], load_sem.at[12]).wait()
    for part in range(2):
        mirror_copy(part).wait()
    own = [fold_sum_rows[pl.ds(t * H, H), :] for t in range(5)]
    seen = [fold_mirror_rows[pl.ds(t * H, H), :] for t in range(5)]
    ends = own[4] + swap64(seen[4])
    local = (
        (own[0] + seen[0], own[1] + seen[1]),
        (own[2] + seen[3], ends),
        (own[3] + seen[2], swap64(ends)),
    )
    for i in range(R):

        def arrived(t):
            return spread_in_rows[pl.ds((t * R + i) * W, W), :]

        top = jnp.concatenate((arrived(0), arrived(2), arrived(3)), axis=0)
        pair = arrived(4)
        end = jnp.concatenate((arrived(1), pair, swap64(pair)), axis=0)
        total = exact_left(merge[...], jnp.concatenate((top, end), axis=1)) + exact_left(
            expand[...], jnp.concatenate(local[i], axis=1)
        )
        dens_out[i] = total[:, :G] * 0.125

    for j in range(R):
        for u in (0, 2, 3):
            wait_bytes(piece_a(out_a, u, j, others), send_a.at[u, j])
        wait_bytes(piece_r(out_r, 1, j, others), send_r.at[1, j])
    wait_bytes(piece_a(out_a, 1, 0, others), send_a.at[1, 0])
    wait_bytes(piece_r(out_r, 0, 0, others), send_r.at[0, 0])
    wait_bytes(row_in.at[others], send_r.at[2, 0])
    wait_bytes(spread_out.at[:, others], send_d.at[5])


def in_hbm(array):
    return pltpu.with_memory_space_constraint(array, pltpu.HBM)


def body(orbitals, responses, energies, weights, potential, perturbation):
    held = [in_hbm(jnp.asarray(table)) for table in tables()]
    anywhere = pl.BlockSpec(memory_space=pl.ANY)
    scalar = pl.BlockSpec(memory_space=pltpu.SMEM)
    vmem, dma = pltpu.VMEM, pltpu.SemaphoreType.DMA
    return pl.pallas_call(
        kernel,
        out_shape=(
            pltpu.VMEM((1, 2, 2, R, G, G), F32),
            pltpu.VMEM((R, G, G), F32),
        ),
        in_specs=[anywhere] * 4 + [scalar] * 2 + [anywhere] * len(held),
        out_specs=(pl.BlockSpec(memory_space=pltpu.VMEM),) * 2,
        scratch_shapes=[vmem(table.shape, BF16) for table in held]
        + [
            vmem((4, 2, R, G, G), F32),
            vmem((R, G, G), F32),
            vmem((R, G, G), F32),
            vmem((4, 9, R, W, 1, 128), F32),
            vmem((4, 9, R, W, 1, 128), F32),
            vmem((2, 9, R, W, 1, 128), F32),
            vmem((2, 9, R, W, 1, 128), F32),
            vmem((R, 3, G, 128), F32),
            vmem((R, 3, G, 128), F32),
            vmem((R, G, 256), F32),
            vmem((5, H, 1, 128), F32),
            vmem((5, H, 1, 128), F32),
            vmem((5, H, 1, 128), F32),
            vmem((5, H, 1, 128), F32),
            vmem((15, W, 1, 128), F32),
            vmem((15, W, 1, 128), F32),
            vmem((8, 8, 128), F32),
            vmem((8, 8, G), F32),
            vmem((1, 128), F32),
            vmem((W, 1, 128), F32),
            dma((13,)),
            dma((14,)),
            dma((4, R)),
            dma((4, R)),
            dma((3, R)),
            dma((3, R)),
            dma((6,)),
            dma((6,)),
        ],
        compiler_params=pltpu.CompilerParams(
            collective_id=0, has_side_effects=True, vmem_limit_bytes=56 * 2**20
        ),
    )(
        in_hbm(orbitals),
        in_hbm(responses),
        in_hbm(jnp.transpose(potential, (1, 0, 2))),
        in_hbm(jnp.transpose(perturbation, (1, 0, 2))),
        energies,
        weights,
        *held,
    )


def solution(mesh):
    placed = (
        P("pool", None, None, "pw", None, None),
        P("pool", None, None, "pw", None, None),
        P("pool", None),
        P("pool"),
        P(None, "pw", None),
        P(None, "pw", None),
    )
    return jax.shard_map(
        body,
        mesh=mesh,
        in_specs=placed,
        out_specs=(P("pool", None, None, "pw", None, None), P("pw", None, None)),
        check_vma=False,
    )
```

```python
import functools
import math

import jax
import jax.numpy as jnp
import ml_dtypes
import numpy as np
from jax import lax
from jax.experimental import pallas as pl
from jax.experimental.pallas import tpu as pltpu
from jax.sharding import PartitionSpec as P

RECIPROCAL_SQUARE = 0.023428
G = 192
W = 64
R = 3
H = 104
C = 14
K = 7 * C
BLOCKS = 27
MESH = pl.DeviceIdType.MESH
F32 = jnp.float32
BF16 = jnp.bfloat16


def halves(table):
    high = table.astype(ml_dtypes.bfloat16)
    low = (table - high.astype(np.float64)).astype(ml_dtypes.bfloat16)
    return [high, low]


def tables():
    index = np.arange(G)
    angles = (np.outer(index, index) % G) * (2.0 * math.pi / G)
    cosine = np.cos(angles) / math.sqrt(G)
    sine = np.sin(angles) / math.sqrt(G)
    spread = np.array([R * (s % W) + s // W for s in range(G)])

    def packed(left, right):
        return np.concatenate(
            (left[:, :128], right[:, :128], left[:, 128:], right[:, 128:]), axis=1
        )

    out_left = np.concatenate((cosine[spread], sine[spread]), axis=0)
    in_left = np.concatenate((cosine[:, spread], sine[:, spread]), axis=0)
    right_real = packed(cosine, sine)
    right_imag = packed(-sine, cosine)
    back_real = packed(cosine, -sine)
    back_imag = packed(sine, cosine)
    back = np.concatenate(
        (back_real[:128], back_imag[:128], back_real[128:], back_imag[128:]), axis=0
    )
    fold = np.zeros((H, G))
    unfold = np.zeros((G, H))
    merge = np.zeros((G, G))
    expand = np.zeros((G, H))
    for a in range(H):
        fold[a, a] += 1.0
        fold[a, -a % G] += 1.0
    for s in range(G):
        a = spread[s]
        unfold[s, min(a, G - a)] = 1.0
        merge[a, s] += 1.0
        merge[-a % G, s] += 1.0
        expand[s, min(s, G - s)] = 1.0
    held = []
    for table in (right_real, right_imag, out_left, in_left, back):
        held += halves(table)
    return held + [m.astype(ml_dtypes.bfloat16) for m in (fold, unfold, merge, expand)]


def split(values):
    high = values.astype(BF16)
    return high, (values - high.astype(F32)).astype(BF16)


def dot(left, right):
    return jnp.dot(left, right, preferred_element_type=F32)


def table_left(high, low, values):
    top, rest = split(values)
    return dot(high, top) + (dot(high, rest) + dot(low, top))


def table_right(values, high, low):
    top, rest = split(values)
    return dot(top, high) + (dot(rest, high) + dot(top, low))


def exact_left(table, values):
    top, rest = split(values)
    last = (values - top.astype(F32) - rest.astype(F32)).astype(BF16)
    return dot(table, top) + (dot(table, rest) + dot(table, last))


def swap64(values):
    return pltpu.roll(values, 64, axis=1)


def lane_sign():
    return jnp.where(lax.broadcasted_iota(jnp.int32, (1, 128), 1) < 64, -1.0, 1.0).astype(F32)


def spin(product, sign):
    cos_part, sin_part = product[:G], product[G:]
    return (
        cos_part[:, :128] - sign * sin_part[:, 128:256],
        cos_part[:, 128:256] + sign * sin_part[:, :128],
        cos_part[:, 256:] + (sign * lane_sign()) * swap64(sin_part[:, 256:]),
    )


def rows_of(start, count):
    if isinstance(start, int):
        return pl.ds(start, count)
    return pl.ds(pl.multiple_of(start, 8), count)


def tiles_at(view, start):
    return jnp.concatenate([view[rows_of(start + t * G, G), :] for t in range(3)], axis=1)


def row_sums(values):
    total = values[0:8]
    for s in range(8, G, 8):
        total = total + values[s : s + 8]
    return total


def squared_freq(index):
    freq = jnp.where(index < G // 2, index, index - G).astype(F32)
    return freq * freq


def kinetic_plane(row):
    plane = squared_freq(lax.broadcasted_iota(jnp.int32, (G, G), 0))
    plane = plane + squared_freq(lax.broadcasted_iota(jnp.int32, (G, G), 1))
    return (0.5 * RECIPROCAL_SQUARE) * (squared_freq(row) + plane)


def kernel(
    orb_hbm, resp_hbm, pot_hbm, pert_hbm, energies, weights, *refs
):
    table_hbm = refs[:14]
    new_out, dens_out = refs[14:16]
    tables_in = refs[16:30]
    (
        raw, pot, pert, out_a, in_a, out_r, in_r, orb_space, app_space, dens,
        fold_mine, fold_other, fold_sum, fold_mirror, spread_out, spread_in,
        sums, sums_g, row_out, row_in,
        load_sem, table_sem, send_a, recv_a, send_r, recv_r, send_d, recv_d,
    ) = refs[30:]
    (wr_h, wr_l, wi_h, wi_l, ol_h, ol_l, il_h, il_l, bk_h, bk_l, fold, unfold, merge, expand) = tables_in

    me = lax.axis_index("pw")
    pool = lax.axis_index("pool")

    def load_table(k):
        return pltpu.make_async_copy(table_hbm[k], tables_in[k], table_sem.at[k])

    def load_unit(u):
        source = orb_hbm if u % 2 == 0 else resp_hbm
        return pltpu.make_async_copy(source.at[0, u // 2], raw.at[u], load_sem.at[u])

    loads_pot = pltpu.make_async_copy(pot_hbm, pot, load_sem.at[4])
    loads_pert = pltpu.make_async_copy(pert_hbm, pert, load_sem.at[5])
    for k in range(4):
        load_table(k).start()
    load_unit(0).start()
    for k in range(4, 6):
        load_table(k).start()
    out_a_rows = out_a.reshape(4 * BLOCKS * W, 128)
    in_a_rows = in_a.reshape(4 * BLOCKS * W, 128)
    out_r_rows = out_r.reshape(2 * BLOCKS * W, 128)
    in_r_rows = in_r.reshape(2 * BLOCKS * W, 128)
    spread_out_rows = spread_out.reshape(15 * W, 128)
    spread_in_rows = spread_in.reshape(15 * W, 128)
    row_in_rows = row_in.reshape(W, 128)
    fold_mine_rows = fold_mine.reshape(5 * H, 128)
    fold_other_rows = fold_other.reshape(5 * H, 128)
    fold_sum_rows = fold_sum.reshape(5 * H, 128)
    fold_mirror_rows = fold_mirror.reshape(5 * H, 128)

    for t in range(5):
        fold_other_rows[pl.ds(t * H + H - 8, 8), :] = jnp.zeros((8, 128), F32)
        fold_mirror_rows[pl.ds(t * H + H - 8, 8), :] = jnp.zeros((8, 128), F32)
    kept = pl.ds(0, K)
    mirrors = ((W - me) % W, W - 1 - me)

    barrier = pltpu.get_barrier_semaphore()

    def peer_at(k):
        return me ^ (1 + (k * 37 + 11) % (W - 1))

    @pl.loop(0, W - 1, unroll=9)
    def _(k):
        pl.semaphore_signal(barrier, inc=1, device_id={"pw": peer_at(k)}, device_id_type=MESH)

    for who in (me, *mirrors):
        pl.semaphore_signal(
            barrier, inc=1, device_id={"pool": 1 - pool, "pw": who}, device_id_type=MESH
        )

    for u in range(1, 4):
        load_unit(u).start()
    for k in range(6, 14):
        load_table(k).start()
    loads_pot.start()
    loads_pert.start()

    for k in range(6):
        load_table(k).wait()

    def piece_a(ref, u, part, who):
        if u == 0:
            return ref.at[u, :, part, who]
        if u == 1:
            return ref.at[u, :, :, who]
        return ref.at[u, pl.ds(3 * part, 3), :, who]

    def send_piece_a(u, part, peer):
        pltpu.make_async_remote_copy(
            src_ref=piece_a(out_a, u, part, peer),
            dst_ref=piece_a(in_a, u, part, me),
            send_sem=send_a.at[u, part],
            recv_sem=recv_a.at[u, part],
            device_id={"pw": peer},
            device_id_type=MESH,
        ).start()

    def wait_bytes(ref, sem):
        pltpu.make_async_copy(ref, ref, sem).wait()

    others = pl.ds(0, W - 1)

    def own_a(u):
        return pltpu.make_async_copy(
            out_a.at[u, :, :, me], in_a.at[u, :, :, me], load_sem.at[6 + u]
        )

    def plane(u, i):
        planes = table_right(raw[u, 0, i], wr_h[...], wr_l[...]) + table_right(
            raw[u, 1, i], wi_h[...], wi_l[...]
        )
        parts = spin(table_left(ol_h[...], ol_l[...], planes), 1.0)
        for j in range(R):
            for t in range(3):
                start = (u * BLOCKS + (j * 3 + t) * R + i) * W
                out_a_rows[rows_of(start, W), :] = parts[t][j * W : (j + 1) * W]

    load_unit(0).wait()
    for i in range(R):
        plane(0, i)
        if i == 0:
            pl.semaphore_wait(barrier, W + 2)

        @pl.loop(0, W - 1, unroll=9)
        def _(k):
            send_piece_a(0, i, peer_at(k))

    own_a(0).start()
    for u in range(1, 4):
        load_unit(u).wait()

        @pl.loop(0, R)
        def _(i):
            plane(u, i)

        if u == 1:

            @pl.loop(0, W - 1, unroll=9)
            def _(k):
                send_piece_a(1, 0, peer_at(k))

        own_a(u).start()

    for j in range(R):

        @pl.loop(0, W - 1, unroll=9)
        def _(k):
            peer = peer_at(k)
            send_piece_a(2, j, peer)
            send_piece_a(3, j, peer)

    for k in range(6, 14):
        load_table(k).wait()

    sums_g[...] = jnp.zeros_like(sums_g)

    @pl.loop(0, R)
    def _(i):
        kinetic = kinetic_plane(R * me + i)
        for n in range(2):
            shifted = kinetic - energies[0, n]
            real = shifted * raw[2 * n + 1, 0, i]
            imag = shifted * raw[2 * n + 1, 1, i]
            for m in range(2):
                left_real, left_imag = raw[2 * m, 0, i], raw[2 * m, 1, i]
                at = (m * 2 + n) * 2
                sums_g[at] += row_sums(left_real * real + left_imag * imag)
                sums_g[at + 1] += row_sums(left_real * imag - left_imag * real)

    loads_pot.wait()
    loads_pert.wait()
    sums[...] = jnp.zeros_like(sums)

    def columns(n, j):
        at = j * 3 * G
        first = 2 * n * BLOCKS * W
        second = (2 * n + 1) * BLOCKS * W
        orb = spin(table_left(il_h[...], il_l[...], tiles_at(in_a_rows, first + at)), 1.0)
        resp = spin(table_left(il_h[...], il_l[...], tiles_at(in_a_rows, second + at)), 1.0)
        pot_top = pot[j, :, 0:128]
        pert_top = pert[j, :, 0:128]
        pot_end = jnp.concatenate((pot[j, :, 128:G], pot[j, :, 128:G]), axis=1)
        pert_end = jnp.concatenate((pert[j, :, 128:G], pert[j, :, 128:G]), axis=1)
        app = (
            pot_top * resp[0] + pert_top * orb[0],
            pot_top * resp[1] + pert_top * orb[1],
            pot_end * resp[2] + pert_end * orb[2],
        )
        ends = orb[2] * resp[2]
        density = (2.0 * weights[0]) * jnp.concatenate(
            (orb[0] * resp[0] + orb[1] * resp[1], ends + swap64(ends)), axis=1
        )

        def overlap(left, right, slot):
            sums[slot] += row_sums(left[0] * right[0] + left[1] * right[1] + left[2] * right[2])
            sums[slot + 1] += row_sums(
                left[0] * right[1]
                - left[1] * right[0]
                - lane_sign() * left[2] * swap64(right[2])
            )

        if n == 0:
            overlap(orb, app, 0)
            dens[j] = density
            for t in range(3):
                orb_space[j, t] = orb[t]
                app_space[j, t] = app[t]
        else:
            dens[j] = dens[j] + density
            orb_first = [orb_space[j, t] for t in range(3)]
            app_first = [app_space[j, t] for t in range(3)]
            overlap(orb_first, app, 2)
            overlap(orb, app_first, 4)
            overlap(orb, app, 6)
        product = table_left(ol_h[...], ol_l[...], jnp.concatenate(app, axis=1))
        turned = jnp.concatenate(spin(product, -1.0), axis=1)
        back = table_right(turned, bk_h[...], bk_l[...])
        for i in range(R):
            for t in range(3):
                start = (n * BLOCKS + (i * 3 + t) * R + j) * W
                out_r_rows[rows_of(start, W), :] = back[
                    i * W : (i + 1) * W, t * 128 : (t + 1) * 128
                ]

    def piece_r(ref, n, part, who):
        if n == 0:
            return ref.at[n, :, :, who]
        return ref.at[n, :, part, who]

    def send_piece_r(n, part, peer):
        pltpu.make_async_remote_copy(
            src_ref=piece_r(out_r, n, part, peer),
            dst_ref=piece_r(in_r, n, part, me),
            send_sem=send_r.at[n, part],
            recv_sem=recv_r.at[n, part],
            device_id={"pw": peer},
            device_id_type=MESH,
        ).start()

    def own_r(n):
        return pltpu.make_async_copy(
            out_r.at[n, :, :, me], in_r.at[n, :, :, me], load_sem.at[10 + n]
        )

    for i in range(R):
        wait_bytes(piece_a(in_a, 0, i, others), recv_a.at[0, i])
    wait_bytes(piece_a(in_a, 1, 0, others), recv_a.at[1, 0])
    own_a(0).wait()
    own_a(1).wait()

    @pl.loop(0, R)
    def _(j):
        columns(0, j)

    @pl.loop(0, W - 1, unroll=9)
    def _(k):
        send_piece_r(0, 0, peer_at(k))

    own_r(0).start()
    own_a(2).wait()
    own_a(3).wait()

    strips_of = ((0, 2), (2, 1), (3, 2))

    def pool_copy(j, rows):
        strips = pl.ds(*strips_of[j])
        return pltpu.make_async_remote_copy(
            src_ref=fold_mine.at[strips, rows],
            dst_ref=fold_other.at[strips, rows],
            send_sem=send_d.at[j],
            recv_sem=recv_d.at[j],
            device_id={"pool": 1 - pool},
            device_id_type=MESH,
        )

    def mirror_copy(j, rows):
        strips = pl.ds(*strips_of[j])
        return pltpu.make_async_remote_copy(
            src_ref=fold_sum.at[strips, rows],
            dst_ref=fold_mirror.at[strips, rows],
            send_sem=send_d.at[3 + j],
            recv_sem=recv_d.at[3 + j],
            device_id={"pool": 1 - pool, "pw": mirrors[min(j, 1)]},
            device_id_type=MESH,
        )

    def piece_d(ref, j, who):
        first, count = strips_of[j]
        return ref.at[pl.ds(3 * first, 3 * count), who]

    def spread(j):
        first, count = strips_of[j]
        pool_copy(j, kept).wait()
        summed = [
            fold_mine_rows[pl.ds(t * H, H), :] + fold_other_rows[pl.ds(t * H, H), :]
            for t in range(first, first + count)
        ]
        for t in range(count):
            fold_sum_rows[pl.ds((first + t) * H, H), :] = summed[t]
        whole = exact_left(unfold[...], jnp.concatenate(summed, axis=1))
        for t in range(count):
            spread_out_rows[pl.ds((first + t) * G, G), :] = whole[:, t * 128 : (t + 1) * 128]

        @pl.loop(0, 7)
        def _(c):
            mirror_copy(j, pl.ds(c * C, C)).start()
            for k in range(9):
                peer = peer_at(c * 9 + k)
                pltpu.make_async_remote_copy(
                    src_ref=piece_d(spread_out, j, peer),
                    dst_ref=piece_d(spread_in, j, me),
                    send_sem=send_d.at[6 + j],
                    recv_sem=recv_d.at[6 + j],
                    device_id={"pw": peer},
                    device_id_type=MESH,
                ).start()

    lane = lax.broadcasted_iota(jnp.int32, (1, 128), 1)
    for j in range(R):
        for u in (2, 3):
            wait_bytes(piece_a(in_a, u, j, others), recv_a.at[u, j])
        columns(1, j)
        if j == 0:
            strips = (dens[0, :, 0:128], dens[0, :, 128:256])
        elif j == 1:
            strips = (dens[1, :, 0:128],)
        else:
            strips = (
                dens[2, :, 0:128],
                jnp.where(lane < 64, dens[1, :, 128:256], dens[2, :, 128:256]),
            )
        first, count = strips_of[j]
        folded = exact_left(fold[...], jnp.concatenate(strips, axis=1))
        for t in range(count):
            fold_mine_rows[pl.ds((first + t) * H, H), :] = folded[:, t * 128 : (t + 1) * 128]

        @pl.loop(0, 7)
        def _(c):
            pool_copy(j, pl.ds(c * C, C)).start()
            for k in range(9):
                send_piece_r(1, j, peer_at(c * 9 + k))

        if j > 0:
            spread(j - 1)

    own_r(1).start()
    row = jnp.zeros((1, 128), F32)
    for k in range(8):
        one = jnp.sum(sums[k], keepdims=True) + jnp.sum(sums_g[k], keepdims=True)
        row = jnp.where(lane == k, one, row)
    row_out[...] = row
    row_in[me] = row

    @pl.loop(0, W - 1, unroll=9)
    def _(k):
        pltpu.make_async_remote_copy(
            src_ref=row_out,
            dst_ref=row_in.at[me],
            send_sem=send_r.at[2, 0],
            recv_sem=recv_r.at[2, 0],
            device_id={"pw": peer_at(k)},
            device_id_type=MESH,
        ).start()

    spread(R - 1)
    pltpu.make_async_copy(spread_out.at[:, me], spread_in.at[:, me], load_sem.at[12]).start()

    wait_bytes(row_in.at[others], recv_r.at[2, 0])
    totals = jnp.sum(row_in_rows[...], axis=0, keepdims=True) * (1.0 / float(G**3))
    inter = [
        jnp.sum(jnp.where(lane == k, totals, 0.0), axis=1, keepdims=True) for k in range(8)
    ]

    def update(n):
        @pl.loop(0, R)
        def _(i):
            parts = tiles_at(in_r_rows, (n * BLOCKS + i * 9) * W)
            app = spin(table_left(il_h[...], il_l[...], parts), -1.0)
            kinetic = kinetic_plane(R * me + i)
            shifted = kinetic - energies[0, n]
            scale = 1.0 / (1.0 + kinetic)
            real = jnp.concatenate((app[0], app[2][:, :64]), axis=1)
            imag = jnp.concatenate((app[1], swap64(app[2])[:, :64]), axis=1)
            resp_real, resp_imag = raw[2 * n + 1, 0, i], raw[2 * n + 1, 1, i]
            real = real + shifted * resp_real
            imag = imag + shifted * resp_imag
            for m in range(2):
                orb_real, orb_imag = raw[2 * m, 0, i], raw[2 * m, 1, i]
                over_real, over_imag = inter[(m * 2 + n) * 2], inter[(m * 2 + n) * 2 + 1]
                real = real - (over_real * orb_real - over_imag * orb_imag)
                imag = imag - (over_imag * orb_real + over_real * orb_imag)
            new_out[0, n, 0, i] = resp_real - real * scale
            new_out[0, n, 1, i] = resp_imag - imag * scale


    wait_bytes(piece_r(in_r, 0, 0, others), recv_r.at[0, 0])
    own_r(0).wait()
    update(0)

    for j in range(R):
        wait_bytes(piece_r(in_r, 1, j, others), recv_r.at[1, j])
    own_r(1).wait()
    update(1)

    for j in range(R):
        wait_bytes(piece_d(spread_in, j, others), recv_d.at[6 + j])
    pltpu.make_async_copy(spread_out.at[:, me], spread_in.at[:, me], load_sem.at[12]).wait()
    for j in range(R):
        mirror_copy(j, kept).wait()
    own = [fold_sum_rows[pl.ds(t * H, H), :] for t in range(5)]
    seen = [fold_mirror_rows[pl.ds(t * H, H), :] for t in range(5)]
    ends = own[4] + swap64(seen[4])
    local = (
        (own[0] + seen[0], own[1] + seen[1]),
        (own[2] + seen[3], ends),
        (own[3] + seen[2], swap64(ends)),
    )
    for i in range(R):

        def arrived(t):
            return spread_in_rows[pl.ds((t * R + i) * W, W), :]

        top = jnp.concatenate((arrived(0), arrived(2), arrived(3)), axis=0)
        pair = arrived(4)
        end = jnp.concatenate((arrived(1), pair, swap64(pair)), axis=0)
        total = exact_left(merge[...], jnp.concatenate((top, end), axis=1)) + exact_left(
            expand[...], jnp.concatenate(local[i], axis=1)
        )
        dens_out[i] = total[:, :G] * 0.125

    for j in range(R):
        for u in (0, 2, 3):
            wait_bytes(piece_a(out_a, u, j, others), send_a.at[u, j])
        wait_bytes(piece_r(out_r, 1, j, others), send_r.at[1, j])
    wait_bytes(piece_a(out_a, 1, 0, others), send_a.at[1, 0])
    wait_bytes(piece_r(out_r, 0, 0, others), send_r.at[0, 0])
    wait_bytes(row_in.at[others], send_r.at[2, 0])
    for j in range(R):
        wait_bytes(piece_d(spread_out, j, others), send_d.at[6 + j])


def in_hbm(array):
    return pltpu.with_memory_space_constraint(array, pltpu.HBM)


def body(orbitals, responses, energies, weights, potential, perturbation):
    held = [in_hbm(jnp.asarray(table)) for table in tables()]
    anywhere = pl.BlockSpec(memory_space=pl.ANY)
    scalar = pl.BlockSpec(memory_space=pltpu.SMEM)
    vmem, dma = pltpu.VMEM, pltpu.SemaphoreType.DMA
    return pl.pallas_call(
        kernel,
        out_shape=(
            pltpu.VMEM((1, 2, 2, R, G, G), F32),
            pltpu.VMEM((R, G, G), F32),
        ),
        in_specs=[anywhere] * 4 + [scalar] * 2 + [anywhere] * len(held),
        out_specs=(pl.BlockSpec(memory_space=pltpu.VMEM),) * 2,
        scratch_shapes=[vmem(table.shape, BF16) for table in held]
        + [
            vmem((4, 2, R, G, G), F32),
            vmem((R, G, G), F32),
            vmem((R, G, G), F32),
            vmem((4, 9, R, W, 1, 128), F32),
            vmem((4, 9, R, W, 1, 128), F32),
            vmem((2, 9, R, W, 1, 128), F32),
            vmem((2, 9, R, W, 1, 128), F32),
            vmem((R, 3, G, 128), F32),
            vmem((R, 3, G, 128), F32),
            vmem((R, G, 256), F32),
            vmem((5, H, 1, 128), F32),
            vmem((5, H, 1, 128), F32),
            vmem((5, H, 1, 128), F32),
            vmem((5, H, 1, 128), F32),
            vmem((15, W, 1, 128), F32),
            vmem((15, W, 1, 128), F32),
            vmem((8, 8, 128), F32),
            vmem((8, 8, G), F32),
            vmem((1, 128), F32),
            vmem((W, 1, 128), F32),
            dma((13,)),
            dma((14,)),
            dma((4, R)),
            dma((4, R)),
            dma((3, R)),
            dma((3, R)),
            dma((9,)),
            dma((9,)),
        ],
        compiler_params=pltpu.CompilerParams(
            collective_id=0, has_side_effects=True, vmem_limit_bytes=56 * 2**20
        ),
    )(
        in_hbm(orbitals),
        in_hbm(responses),
        in_hbm(jnp.transpose(potential, (1, 0, 2))),
        in_hbm(jnp.transpose(perturbation, (1, 0, 2))),
        energies,
        weights,
        *held,
    )


def solution(mesh):
    placed = (
        P("pool", None, None, "pw", None, None),
        P("pool", None, None, "pw", None, None),
        P("pool", None),
        P("pool"),
        P(None, "pw", None),
        P(None, "pw", None),
    )
    return jax.shard_map(
        body,
        mesh=mesh,
        in_specs=placed,
        out_specs=(P("pool", None, None, "pw", None, None), P("pw", None, None)),
        check_vma=False,
    )
```

```python
import functools
import math

import jax
import jax.numpy as jnp
import ml_dtypes
import numpy as np
from jax import lax
from jax.experimental import pallas as pl
from jax.experimental.pallas import tpu as pltpu
from jax.sharding import PartitionSpec as P

RECIPROCAL_SQUARE = 0.023428
G = 192
W = 64
R = 3
H = 104
C = 14
K = 7 * C
BLOCKS = 27
MESH = pl.DeviceIdType.MESH
F32 = jnp.float32
BF16 = jnp.bfloat16


def halves(table):
    high = table.astype(ml_dtypes.bfloat16)
    low = (table - high.astype(np.float64)).astype(ml_dtypes.bfloat16)
    return [high, low]


def tables():
    index = np.arange(G)
    angles = (np.outer(index, index) % G) * (2.0 * math.pi / G)
    cosine = np.cos(angles) / math.sqrt(G)
    sine = np.sin(angles) / math.sqrt(G)
    spread = np.array([R * (s % W) + s // W for s in range(G)])

    def packed(left, right):
        return np.concatenate(
            (left[:, :128], right[:, :128], left[:, 128:], right[:, 128:]), axis=1
        )

    out_left = np.concatenate((cosine[spread], sine[spread]), axis=0)
    in_left = np.concatenate((cosine[:, spread], sine[:, spread]), axis=0)
    right_real = packed(cosine, sine)
    right_imag = packed(-sine, cosine)
    back_real = packed(cosine, -sine)
    back_imag = packed(sine, cosine)
    back = np.concatenate(
        (back_real[:128], back_imag[:128], back_real[128:], back_imag[128:]), axis=0
    )
    fold = np.zeros((H, G))
    unfold = np.zeros((G, H))
    merge = np.zeros((G, G))
    expand = np.zeros((G, H))
    for a in range(H):
        fold[a, a] += 1.0
        fold[a, -a % G] += 1.0
    for s in range(G):
        a = spread[s]
        unfold[s, min(a, G - a)] = 1.0
        merge[a, s] += 1.0
        merge[-a % G, s] += 1.0
        expand[s, min(s, G - s)] = 1.0
    held = []
    for table in (right_real, right_imag, out_left, in_left, back):
        held += halves(table)
    return held + [m.astype(ml_dtypes.bfloat16) for m in (fold, unfold, merge, expand)]


def split(values):
    high = values.astype(BF16)
    return high, (values - high.astype(F32)).astype(BF16)


def dot(left, right):
    return jnp.dot(left, right, preferred_element_type=F32)


def table_left(high, low, values):
    top, rest = split(values)
    return dot(high, top) + (dot(high, rest) + dot(low, top))


def table_right(values, high, low):
    top, rest = split(values)
    return dot(top, high) + (dot(rest, high) + dot(top, low))


def exact_left(table, values):
    top, rest = split(values)
    last = (values - top.astype(F32) - rest.astype(F32)).astype(BF16)
    return dot(table, top) + (dot(table, rest) + dot(table, last))


def swap64(values):
    return pltpu.roll(values, 64, axis=1)


def lane_sign():
    return jnp.where(lax.broadcasted_iota(jnp.int32, (1, 128), 1) < 64, -1.0, 1.0).astype(F32)


def spin(product, sign):
    cos_part, sin_part = product[:G], product[G:]
    return (
        cos_part[:, :128] - sign * sin_part[:, 128:256],
        cos_part[:, 128:256] + sign * sin_part[:, :128],
        cos_part[:, 256:] + (sign * lane_sign()) * swap64(sin_part[:, 256:]),
    )


def rows_of(start, count):
    if isinstance(start, int):
        return pl.ds(start, count)
    return pl.ds(pl.multiple_of(start, 8), count)


def tiles_at(view, start):
    return jnp.concatenate([view[rows_of(start + t * G, G), :] for t in range(3)], axis=1)


def row_sums(values):
    total = values[0:8]
    for s in range(8, G, 8):
        total = total + values[s : s + 8]
    return total


def squared_freq(index):
    freq = jnp.where(index < G // 2, index, index - G).astype(F32)
    return freq * freq


def kinetic_plane(row):
    plane = squared_freq(lax.broadcasted_iota(jnp.int32, (G, G), 0))
    plane = plane + squared_freq(lax.broadcasted_iota(jnp.int32, (G, G), 1))
    return (0.5 * RECIPROCAL_SQUARE) * (squared_freq(row) + plane)


def kernel(
    orb_hbm, resp_hbm, pot_hbm, pert_hbm, energies, weights, *refs
):
    table_hbm = refs[:14]
    new_out, dens_out = refs[14:16]
    tables_in = refs[16:30]
    (
        raw, pot, pert, out_a, in_a, out_r, in_r, orb_space, app_space, dens,
        fold_mine, fold_other, fold_sum, fold_mirror, spread_out, spread_in,
        sums, sums_g, row_out, row_in,
        load_sem, table_sem, send_a, recv_a, send_r, recv_r, send_d, recv_d,
    ) = refs[30:]
    (wr_h, wr_l, wi_h, wi_l, ol_h, ol_l, il_h, il_l, bk_h, bk_l, fold, unfold, merge, expand) = tables_in

    me = lax.axis_index("pw")
    pool = lax.axis_index("pool")

    def load_table(k):
        return pltpu.make_async_copy(table_hbm[k], tables_in[k], table_sem.at[k])

    def load_unit(u):
        source = orb_hbm if u % 2 == 0 else resp_hbm
        return pltpu.make_async_copy(source.at[0, u // 2], raw.at[u], load_sem.at[u])

    loads_pot = pltpu.make_async_copy(pot_hbm, pot, load_sem.at[4])
    loads_pert = pltpu.make_async_copy(pert_hbm, pert, load_sem.at[5])
    for k in range(4):
        load_table(k).start()
    load_unit(0).start()
    for k in range(4, 6):
        load_table(k).start()
    out_a_rows = out_a.reshape(4 * BLOCKS * W, 128)
    in_a_rows = in_a.reshape(4 * BLOCKS * W, 128)
    out_r_rows = out_r.reshape(2 * BLOCKS * W, 128)
    in_r_rows = in_r.reshape(2 * BLOCKS * W, 128)
    spread_out_rows = spread_out.reshape(15 * W, 128)
    spread_in_rows = spread_in.reshape(15 * W, 128)
    row_in_rows = row_in.reshape(W, 128)
    fold_mine_rows = fold_mine.reshape(5 * H, 128)
    fold_other_rows = fold_other.reshape(5 * H, 128)
    fold_sum_rows = fold_sum.reshape(5 * H, 128)
    fold_mirror_rows = fold_mirror.reshape(5 * H, 128)

    for t in range(5):
        fold_other_rows[pl.ds(t * H + H - 8, 8), :] = jnp.zeros((8, 128), F32)
        fold_mirror_rows[pl.ds(t * H + H - 8, 8), :] = jnp.zeros((8, 128), F32)
    kept = pl.ds(0, K)
    mirrors = ((W - me) % W, W - 1 - me)

    barrier = pltpu.get_barrier_semaphore()

    def peer_at(k):
        return me ^ (1 + (k * 37 + 11) % (W - 1))

    @pl.loop(0, W - 1, unroll=9)
    def _(k):
        pl.semaphore_signal(barrier, inc=1, device_id={"pw": peer_at(k)}, device_id_type=MESH)

    for who in (me, *mirrors):
        pl.semaphore_signal(
            barrier, inc=1, device_id={"pool": 1 - pool, "pw": who}, device_id_type=MESH
        )

    for u in range(1, 4):
        load_unit(u).start()
    for k in range(6, 14):
        load_table(k).start()
    loads_pot.start()
    loads_pert.start()

    for k in range(6):
        load_table(k).wait()

    def piece_a(ref, u, part, who):
        if u == 0:
            return ref.at[u, :, part, who]
        if u == 1:
            return ref.at[u, :, :, who]
        return ref.at[u, pl.ds(3 * part, 3), :, who]

    def send_piece_a(u, part, peer):
        pltpu.make_async_remote_copy(
            src_ref=piece_a(out_a, u, part, peer),
            dst_ref=piece_a(in_a, u, part, me),
            send_sem=send_a.at[u, part],
            recv_sem=recv_a.at[u, part],
            device_id={"pw": peer},
            device_id_type=MESH,
        ).start()

    def wait_bytes(ref, sem):
        pltpu.make_async_copy(ref, ref, sem).wait()

    others = pl.ds(0, W - 1)

    def own_a(u):
        return pltpu.make_async_copy(
            out_a.at[u, :, :, me], in_a.at[u, :, :, me], load_sem.at[6 + u]
        )

    def plane(u, i):
        planes = table_right(raw[u, 0, i], wr_h[...], wr_l[...]) + table_right(
            raw[u, 1, i], wi_h[...], wi_l[...]
        )
        parts = spin(table_left(ol_h[...], ol_l[...], planes), 1.0)
        for j in range(R):
            for t in range(3):
                start = (u * BLOCKS + (j * 3 + t) * R + i) * W
                out_a_rows[rows_of(start, W), :] = parts[t][j * W : (j + 1) * W]

    load_unit(0).wait()
    for i in range(R):
        plane(0, i)
        if i == 0:
            pl.semaphore_wait(barrier, W + 2)

        @pl.loop(0, W - 1, unroll=9)
        def _(k):
            send_piece_a(0, i, peer_at(k))

    own_a(0).start()
    for u in range(1, 4):
        load_unit(u).wait()

        @pl.loop(0, R)
        def _(i):
            plane(u, i)

        if u == 1:

            @pl.loop(0, W - 1, unroll=9)
            def _(k):
                send_piece_a(1, 0, peer_at(k))

        own_a(u).start()

    for j in range(R):

        @pl.loop(0, W - 1, unroll=9)
        def _(k):
            peer = peer_at(k)
            send_piece_a(2, j, peer)
            send_piece_a(3, j, peer)

    for k in range(6, 14):
        load_table(k).wait()

    sums_g[...] = jnp.zeros_like(sums_g)

    @pl.loop(0, R)
    def _(i):
        kinetic = kinetic_plane(R * me + i)
        for n in range(2):
            shifted = kinetic - energies[0, n]
            real = shifted * raw[2 * n + 1, 0, i]
            imag = shifted * raw[2 * n + 1, 1, i]
            for m in range(2):
                left_real, left_imag = raw[2 * m, 0, i], raw[2 * m, 1, i]
                at = (m * 2 + n) * 2
                sums_g[at] += row_sums(left_real * real + left_imag * imag)
                sums_g[at + 1] += row_sums(left_real * imag - left_imag * real)

    loads_pot.wait()
    loads_pert.wait()
    sums[...] = jnp.zeros_like(sums)

    def columns(n, j):
        at = j * 3 * G
        first = 2 * n * BLOCKS * W
        second = (2 * n + 1) * BLOCKS * W
        orb = spin(table_left(il_h[...], il_l[...], tiles_at(in_a_rows, first + at)), 1.0)
        resp = spin(table_left(il_h[...], il_l[...], tiles_at(in_a_rows, second + at)), 1.0)
        pot_top = pot[j, :, 0:128]
        pert_top = pert[j, :, 0:128]
        pot_end = jnp.concatenate((pot[j, :, 128:G], pot[j, :, 128:G]), axis=1)
        pert_end = jnp.concatenate((pert[j, :, 128:G], pert[j, :, 128:G]), axis=1)
        app = (
            pot_top * resp[0] + pert_top * orb[0],
            pot_top * resp[1] + pert_top * orb[1],
            pot_end * resp[2] + pert_end * orb[2],
        )
        ends = orb[2] * resp[2]
        density = (2.0 * weights[0]) * jnp.concatenate(
            (orb[0] * resp[0] + orb[1] * resp[1], ends + swap64(ends)), axis=1
        )

        def overlap(left, right, slot):
            sums[slot] += row_sums(left[0] * right[0] + left[1] * right[1] + left[2] * right[2])
            sums[slot + 1] += row_sums(
                left[0] * right[1]
                - left[1] * right[0]
                - lane_sign() * left[2] * swap64(right[2])
            )

        if n == 0:
            overlap(orb, app, 0)
            dens[j] = density
            for t in range(3):
                orb_space[j, t] = orb[t]
                app_space[j, t] = app[t]
        else:
            dens[j] = dens[j] + density
            orb_first = [orb_space[j, t] for t in range(3)]
            app_first = [app_space[j, t] for t in range(3)]
            overlap(orb_first, app, 2)
            overlap(orb, app_first, 4)
            overlap(orb, app, 6)
        product = table_left(ol_h[...], ol_l[...], jnp.concatenate(app, axis=1))
        turned = jnp.concatenate(spin(product, -1.0), axis=1)
        back = table_right(turned, bk_h[...], bk_l[...])
        for i in range(R):
            for t in range(3):
                start = (n * BLOCKS + (i * 3 + t) * R + j) * W
                out_r_rows[rows_of(start, W), :] = back[
                    i * W : (i + 1) * W, t * 128 : (t + 1) * 128
                ]

    def piece_r(ref, n, part, who):
        if n == 0:
            return ref.at[n, :, :, who]
        return ref.at[n, :, part, who]

    def send_piece_r(n, part, peer):
        pltpu.make_async_remote_copy(
            src_ref=piece_r(out_r, n, part, peer),
            dst_ref=piece_r(in_r, n, part, me),
            send_sem=send_r.at[n, part],
            recv_sem=recv_r.at[n, part],
            device_id={"pw": peer},
            device_id_type=MESH,
        ).start()

    def own_r(n):
        return pltpu.make_async_copy(
            out_r.at[n, :, :, me], in_r.at[n, :, :, me], load_sem.at[10 + n]
        )

    for i in range(R):
        wait_bytes(piece_a(in_a, 0, i, others), recv_a.at[0, i])
    wait_bytes(piece_a(in_a, 1, 0, others), recv_a.at[1, 0])
    own_a(0).wait()
    own_a(1).wait()

    @pl.loop(0, R)
    def _(j):
        columns(0, j)

    @pl.loop(0, W - 1, unroll=9)
    def _(k):
        send_piece_r(0, 0, peer_at(k))

    own_r(0).start()
    own_a(2).wait()
    own_a(3).wait()

    strips_of = ((0, 2), (2, 1), (3, 2))

    def pool_copy(j, rows):
        strips = pl.ds(*strips_of[j])
        return pltpu.make_async_remote_copy(
            src_ref=fold_mine.at[strips, rows],
            dst_ref=fold_other.at[strips, rows],
            send_sem=send_d.at[j],
            recv_sem=recv_d.at[j],
            device_id={"pool": 1 - pool},
            device_id_type=MESH,
        )

    def mirror_copy(j, rows):
        strips = pl.ds(*strips_of[j])
        return pltpu.make_async_remote_copy(
            src_ref=fold_sum.at[strips, rows],
            dst_ref=fold_mirror.at[strips, rows],
            send_sem=send_d.at[3 + j],
            recv_sem=recv_d.at[3 + j],
            device_id={"pool": 1 - pool, "pw": mirrors[min(j, 1)]},
            device_id_type=MESH,
        )

    def piece_d(ref, j, who):
        first, count = strips_of[j]
        return ref.at[pl.ds(3 * first, 3 * count), who]

    def spread(j):
        first, count = strips_of[j]
        pool_copy(j, kept).wait()
        summed = [
            fold_mine_rows[pl.ds(t * H, H), :] + fold_other_rows[pl.ds(t * H, H), :]
            for t in range(first, first + count)
        ]
        for t in range(count):
            fold_sum_rows[pl.ds((first + t) * H, H), :] = summed[t]
        whole = exact_left(unfold[...], jnp.concatenate(summed, axis=1))
        for t in range(count):
            spread_out_rows[pl.ds((first + t) * G, G), :] = whole[:, t * 128 : (t + 1) * 128]

        @pl.loop(0, 7)
        def _(c):
            mirror_copy(j, pl.ds(c * C, C)).start()
            for k in range(9):
                peer = peer_at(c * 9 + k)
                pltpu.make_async_remote_copy(
                    src_ref=piece_d(spread_out, j, peer),
                    dst_ref=piece_d(spread_in, j, me),
                    send_sem=send_d.at[6 + j],
                    recv_sem=recv_d.at[6 + j],
                    device_id={"pw": peer},
                    device_id_type=MESH,
                ).start()

    lane = lax.broadcasted_iota(jnp.int32, (1, 128), 1)
    for j in range(R):
        for u in (2, 3):
            wait_bytes(piece_a(in_a, u, j, others), recv_a.at[u, j])
        columns(1, j)
        if j == 0:
            strips = (dens[0, :, 0:128], dens[0, :, 128:256])
        elif j == 1:
            strips = (dens[1, :, 0:128],)
        else:
            strips = (
                dens[2, :, 0:128],
                jnp.where(lane < 64, dens[1, :, 128:256], dens[2, :, 128:256]),
            )
        first, count = strips_of[j]
        folded = exact_left(fold[...], jnp.concatenate(strips, axis=1))
        for t in range(count):
            fold_mine_rows[pl.ds((first + t) * H, H), :] = folded[:, t * 128 : (t + 1) * 128]

        @pl.loop(0, 7)
        def _(c):
            pool_copy(j, pl.ds(c * C, C)).start()
            for k in range(9):
                send_piece_r(1, j, peer_at(c * 9 + k))

        if j > 0:
            spread(j - 1)

    own_r(1).start()
    row = jnp.zeros((1, 128), F32)
    for k in range(8):
        one = jnp.sum(sums[k], keepdims=True) + jnp.sum(sums_g[k], keepdims=True)
        row = jnp.where(lane == k, one, row)
    row_out[...] = row
    row_in[me] = row

    @pl.loop(0, W - 1, unroll=9)
    def _(k):
        pltpu.make_async_remote_copy(
            src_ref=row_out,
            dst_ref=row_in.at[me],
            send_sem=send_r.at[2, 0],
            recv_sem=recv_r.at[2, 0],
            device_id={"pw": peer_at(k)},
            device_id_type=MESH,
        ).start()

    spread(R - 1)
    pltpu.make_async_copy(spread_out.at[:, me], spread_in.at[:, me], load_sem.at[12]).start()

    wait_bytes(row_in.at[others], recv_r.at[2, 0])
    totals = jnp.sum(row_in_rows[...], axis=0, keepdims=True) * (1.0 / float(G**3))
    inter = [
        jnp.sum(jnp.where(lane == k, totals, 0.0), axis=1, keepdims=True) for k in range(8)
    ]

    def update(n):
        @pl.loop(0, R)
        def _(i):
            parts = tiles_at(in_r_rows, (n * BLOCKS + i * 9) * W)
            app = spin(table_left(il_h[...], il_l[...], parts), -1.0)
            kinetic = kinetic_plane(R * me + i)
            shifted = kinetic - energies[0, n]
            scale = 1.0 / (1.0 + kinetic)
            real = jnp.concatenate((app[0], app[2][:, :64]), axis=1)
            imag = jnp.concatenate((app[1], swap64(app[2])[:, :64]), axis=1)
            resp_real, resp_imag = raw[2 * n + 1, 0, i], raw[2 * n + 1, 1, i]
            real = real + shifted * resp_real
            imag = imag + shifted * resp_imag
            for m in range(2):
                orb_real, orb_imag = raw[2 * m, 0, i], raw[2 * m, 1, i]
                over_real, over_imag = inter[(m * 2 + n) * 2], inter[(m * 2 + n) * 2 + 1]
                real = real - (over_real * orb_real - over_imag * orb_imag)
                imag = imag - (over_imag * orb_real + over_real * orb_imag)
            new_out[0, n, 0, i] = resp_real - real * scale
            new_out[0, n, 1, i] = resp_imag - imag * scale


    wait_bytes(piece_r(in_r, 0, 0, others), recv_r.at[0, 0])
    own_r(0).wait()
    update(0)

    for j in range(R):
        wait_bytes(piece_r(in_r, 1, j, others), recv_r.at[1, j])
    own_r(1).wait()
    update(1)

    for j in range(R):
        wait_bytes(piece_d(spread_in, j, others), recv_d.at[6 + j])
    pltpu.make_async_copy(spread_out.at[:, me], spread_in.at[:, me], load_sem.at[12]).wait()
    for j in range(R):
        mirror_copy(j, kept).wait()
    own = [fold_sum_rows[pl.ds(t * H, H), :] for t in range(5)]
    seen = [fold_mirror_rows[pl.ds(t * H, H), :] for t in range(5)]
    ends = own[4] + swap64(seen[4])
    local = (
        (own[0] + seen[0], own[1] + seen[1]),
        (own[2] + seen[3], ends),
        (own[3] + seen[2], swap64(ends)),
    )
    for i in range(R):

        def arrived(t):
            return spread_in_rows[pl.ds((t * R + i) * W, W), :]

        top = jnp.concatenate((arrived(0), arrived(2), arrived(3)), axis=0)
        pair = arrived(4)
        end = jnp.concatenate((arrived(1), pair, swap64(pair)), axis=0)
        total = exact_left(merge[...], jnp.concatenate((top, end), axis=1)) + exact_left(
            expand[...], jnp.concatenate(local[i], axis=1)
        )
        dens_out[i] = total[:, :G] * 0.125

    for j in range(R):
        for u in (0, 2, 3):
            wait_bytes(piece_a(out_a, u, j, others), send_a.at[u, j])
        wait_bytes(piece_r(out_r, 1, j, others), send_r.at[1, j])
    wait_bytes(piece_a(out_a, 1, 0, others), send_a.at[1, 0])
    wait_bytes(piece_r(out_r, 0, 0, others), send_r.at[0, 0])
    wait_bytes(row_in.at[others], send_r.at[2, 0])
    for j in range(R):
        wait_bytes(piece_d(spread_out, j, others), send_d.at[6 + j])


def store(new_vmem, dens_vmem, new_hbm, dens_hbm, sem):
    copies = [
        pltpu.make_async_copy(new_vmem.at[0, n, c], new_hbm.at[0, n, c], sem.at[2 * n + c])
        for n in range(2)
        for c in range(2)
    ]
    copies.append(pltpu.make_async_copy(dens_vmem, dens_hbm, sem.at[4]))
    for copy in copies:
        copy.start()
    for copy in copies:
        copy.wait()


def in_hbm(array):
    return pltpu.with_memory_space_constraint(array, pltpu.HBM)


def body(orbitals, responses, energies, weights, potential, perturbation):
    held = [in_hbm(jnp.asarray(table)) for table in tables()]
    anywhere = pl.BlockSpec(memory_space=pl.ANY)
    scalar = pl.BlockSpec(memory_space=pltpu.SMEM)
    vmem, dma = pltpu.VMEM, pltpu.SemaphoreType.DMA
    results = pl.pallas_call(
        kernel,
        out_shape=(
            pltpu.VMEM((1, 2, 2, R, G, G), F32),
            pltpu.VMEM((R, G, G), F32),
        ),
        in_specs=[anywhere] * 4 + [scalar] * 2 + [anywhere] * len(held),
        out_specs=(pl.BlockSpec(memory_space=pltpu.VMEM),) * 2,
        scratch_shapes=[vmem(table.shape, BF16) for table in held]
        + [
            vmem((4, 2, R, G, G), F32),
            vmem((R, G, G), F32),
            vmem((R, G, G), F32),
            vmem((4, 9, R, W, 1, 128), F32),
            vmem((4, 9, R, W, 1, 128), F32),
            vmem((2, 9, R, W, 1, 128), F32),
            vmem((2, 9, R, W, 1, 128), F32),
            vmem((R, 3, G, 128), F32),
            vmem((R, 3, G, 128), F32),
            vmem((R, G, 256), F32),
            vmem((5, H, 1, 128), F32),
            vmem((5, H, 1, 128), F32),
            vmem((5, H, 1, 128), F32),
            vmem((5, H, 1, 128), F32),
            vmem((15, W, 1, 128), F32),
            vmem((15, W, 1, 128), F32),
            vmem((8, 8, 128), F32),
            vmem((8, 8, G), F32),
            vmem((1, 128), F32),
            vmem((W, 1, 128), F32),
            dma((13,)),
            dma((14,)),
            dma((4, R)),
            dma((4, R)),
            dma((3, R)),
            dma((3, R)),
            dma((9,)),
            dma((9,)),
        ],
        compiler_params=pltpu.CompilerParams(
            collective_id=0, has_side_effects=True, vmem_limit_bytes=56 * 2**20
        ),
    )(
        in_hbm(orbitals),
        in_hbm(responses),
        in_hbm(jnp.transpose(potential, (1, 0, 2))),
        in_hbm(jnp.transpose(perturbation, (1, 0, 2))),
        energies,
        weights,
        *held,
    )
    return pl.pallas_call(
        store,
        out_shape=(
            jax.ShapeDtypeStruct((1, 2, 2, R, G, G), F32),
            jax.ShapeDtypeStruct((R, G, G), F32),
        ),
        in_specs=[pl.BlockSpec(memory_space=pltpu.VMEM)] * 2,
        out_specs=(anywhere, anywhere),
        scratch_shapes=[dma((5,))],
    )(*(pltpu.with_memory_space_constraint(result, pltpu.VMEM) for result in results))


def solution(mesh):
    placed = (
        P("pool", None, None, "pw", None, None),
        P("pool", None, None, "pw", None, None),
        P("pool", None),
        P("pool"),
        P(None, "pw", None),
        P(None, "pw", None),
    )
    return jax.shard_map(
        body,
        mesh=mesh,
        in_specs=placed,
        out_specs=(P("pool", None, None, "pw", None, None), P("pw", None, None)),
        check_vma=False,
    )
```

```python
import functools
import math

import jax
import jax.numpy as jnp
import ml_dtypes
import numpy as np
from jax import lax
from jax.experimental import pallas as pl
from jax.experimental.pallas import tpu as pltpu
from jax.sharding import PartitionSpec as P

RECIPROCAL_SQUARE = 0.023428
G = 192
W = 64
R = 3
H = 104
C = 14
K = 7 * C
BLOCKS = 27
MESH = pl.DeviceIdType.MESH
F32 = jnp.float32
BF16 = jnp.bfloat16


def halves(table):
    high = table.astype(ml_dtypes.bfloat16)
    low = (table - high.astype(np.float64)).astype(ml_dtypes.bfloat16)
    return [high, low]


def tables():
    index = np.arange(G)
    angles = (np.outer(index, index) % G) * (2.0 * math.pi / G)
    cosine = np.cos(angles) / math.sqrt(G)
    sine = np.sin(angles) / math.sqrt(G)
    spread = np.array([R * (s % W) + s // W for s in range(G)])

    def packed(left, right):
        return np.concatenate(
            (left[:, :128], right[:, :128], left[:, 128:], right[:, 128:]), axis=1
        )

    out_left = np.concatenate((cosine[spread], sine[spread]), axis=0)
    in_left = np.concatenate((cosine[:, spread], sine[:, spread]), axis=0)
    right_real = packed(cosine, sine)
    right_imag = packed(-sine, cosine)
    back_real = packed(cosine, -sine)
    back_imag = packed(sine, cosine)
    back = np.concatenate(
        (back_real[:128], back_imag[:128], back_real[128:], back_imag[128:]), axis=0
    )
    fold = np.zeros((H, G))
    unfold = np.zeros((G, H))
    merge = np.zeros((G, G))
    expand = np.zeros((G, H))
    for a in range(H):
        fold[a, a] += 1.0
        fold[a, -a % G] += 1.0
    for s in range(G):
        a = spread[s]
        unfold[s, min(a, G - a)] = 1.0
        merge[a, s] += 1.0
        merge[-a % G, s] += 1.0
        expand[s, min(s, G - s)] = 1.0
    held = []
    for table in (right_real, right_imag, out_left, in_left, back):
        held += halves(table)
    return held + [m.astype(ml_dtypes.bfloat16) for m in (fold, unfold, merge, expand)]


def split(values):
    high = values.astype(BF16)
    return high, (values - high.astype(F32)).astype(BF16)


def dot(left, right):
    return jnp.dot(left, right, preferred_element_type=F32)


def table_left(high, low, values):
    top, rest = split(values)
    return dot(high, top) + (dot(high, rest) + dot(low, top))


def table_right(values, high, low):
    top, rest = split(values)
    return dot(top, high) + (dot(rest, high) + dot(top, low))


def exact_left(table, values):
    top, rest = split(values)
    last = (values - top.astype(F32) - rest.astype(F32)).astype(BF16)
    return dot(table, top) + (dot(table, rest) + dot(table, last))


def swap64(values):
    return pltpu.roll(values, 64, axis=1)


def lane_sign():
    return jnp.where(lax.broadcasted_iota(jnp.int32, (1, 128), 1) < 64, -1.0, 1.0).astype(F32)


def spin(product, sign):
    cos_part, sin_part = product[:G], product[G:]
    return (
        cos_part[:, :128] - sign * sin_part[:, 128:256],
        cos_part[:, 128:256] + sign * sin_part[:, :128],
        cos_part[:, 256:] + (sign * lane_sign()) * swap64(sin_part[:, 256:]),
    )


def rows_of(start, count):
    if isinstance(start, int):
        return pl.ds(start, count)
    return pl.ds(pl.multiple_of(start, 8), count)


def tiles_at(view, start):
    return jnp.concatenate([view[rows_of(start + t * G, G), :] for t in range(3)], axis=1)


def row_sums(values):
    total = values[0:8]
    for s in range(8, G, 8):
        total = total + values[s : s + 8]
    return total


def squared_freq(index):
    freq = jnp.where(index < G // 2, index, index - G).astype(F32)
    return freq * freq


def kinetic_plane(row):
    plane = squared_freq(lax.broadcasted_iota(jnp.int32, (G, G), 0))
    plane = plane + squared_freq(lax.broadcasted_iota(jnp.int32, (G, G), 1))
    return (0.5 * RECIPROCAL_SQUARE) * (squared_freq(row) + plane)


def kernel(
    orb_hbm, resp_hbm, pot_hbm, pert_hbm, energies, weights, *refs
):
    table_hbm = refs[:14]
    new_out, dens_out = refs[14:16]
    tables_in = refs[16:30]
    (
        raw, pot, pert, out_a, in_a, out_r, in_r, orb_space, app_space, dens,
        fold_mine, fold_other, fold_sum, fold_mirror, spread_out, spread_in,
        sums, sums_g, row_out, row_in,
        load_sem, table_sem, send_a, recv_a, send_r, recv_r, send_d, recv_d,
    ) = refs[30:]
    (wr_h, wr_l, wi_h, wi_l, ol_h, ol_l, il_h, il_l, bk_h, bk_l, fold, unfold, merge, expand) = tables_in

    me = lax.axis_index("pw")
    pool = lax.axis_index("pool")

    def load_table(k):
        return pltpu.make_async_copy(table_hbm[k], tables_in[k], table_sem.at[k])

    def load_unit(u):
        source = orb_hbm if u % 2 == 0 else resp_hbm
        return pltpu.make_async_copy(source.at[0, u // 2], raw.at[u], load_sem.at[u])

    loads_pot = pltpu.make_async_copy(pot_hbm, pot, load_sem.at[4])
    loads_pert = pltpu.make_async_copy(pert_hbm, pert, load_sem.at[5])
    for k in range(4):
        load_table(k).start()
    load_unit(0).start()
    for k in range(4, 6):
        load_table(k).start()
    out_a_rows = out_a.reshape(4 * BLOCKS * W, 128)
    in_a_rows = in_a.reshape(4 * BLOCKS * W, 128)
    out_r_rows = out_r.reshape(2 * BLOCKS * W, 128)
    in_r_rows = in_r.reshape(2 * BLOCKS * W, 128)
    spread_out_rows = spread_out.reshape(15 * W, 128)
    spread_in_rows = spread_in.reshape(15 * W, 128)
    row_in_rows = row_in.reshape(W, 128)
    fold_mine_rows = fold_mine.reshape(5 * H, 128)
    fold_other_rows = fold_other.reshape(5 * H, 128)
    fold_sum_rows = fold_sum.reshape(5 * H, 128)
    fold_mirror_rows = fold_mirror.reshape(5 * H, 128)

    for t in range(5):
        fold_other_rows[pl.ds(t * H + H - 8, 8), :] = jnp.zeros((8, 128), F32)
        fold_mirror_rows[pl.ds(t * H + H - 8, 8), :] = jnp.zeros((8, 128), F32)
    kept = pl.ds(0, K)
    mirrors = ((W - me) % W, W - 1 - me)

    barrier = pltpu.get_barrier_semaphore()

    def peer_at(k):
        return me ^ (1 + (k * 37 + 11) % (W - 1))

    @pl.loop(0, W - 1, unroll=9)
    def _(k):
        pl.semaphore_signal(barrier, inc=1, device_id={"pw": peer_at(k)}, device_id_type=MESH)

    for who in (me, *mirrors):
        pl.semaphore_signal(
            barrier, inc=1, device_id={"pool": 1 - pool, "pw": who}, device_id_type=MESH
        )

    for u in range(1, 4):
        load_unit(u).start()
    for k in range(6, 14):
        load_table(k).start()
    loads_pot.start()
    loads_pert.start()

    for k in range(6):
        load_table(k).wait()

    def piece_a(ref, u, part, who):
        if u == 0:
            return ref.at[u, :, part, who]
        if u == 1:
            return ref.at[u, :, :, who]
        return ref.at[u, pl.ds(3 * part, 3), :, who]

    def send_piece_a(u, part, peer):
        pltpu.make_async_remote_copy(
            src_ref=piece_a(out_a, u, part, peer),
            dst_ref=piece_a(in_a, u, part, me),
            send_sem=send_a.at[u, part],
            recv_sem=recv_a.at[u, part],
            device_id={"pw": peer},
            device_id_type=MESH,
        ).start()

    def wait_bytes(ref, sem):
        pltpu.make_async_copy(ref, ref, sem).wait()

    others = pl.ds(0, W - 1)

    def own_a(u):
        return pltpu.make_async_copy(
            out_a.at[u, :, :, me], in_a.at[u, :, :, me], load_sem.at[6 + u]
        )

    def plane(u, i):
        planes = table_right(raw[u, 0, i], wr_h[...], wr_l[...]) + table_right(
            raw[u, 1, i], wi_h[...], wi_l[...]
        )
        parts = spin(table_left(ol_h[...], ol_l[...], planes), 1.0)
        for j in range(R):
            for t in range(3):
                start = (u * BLOCKS + (j * 3 + t) * R + i) * W
                out_a_rows[rows_of(start, W), :] = parts[t][j * W : (j + 1) * W]

    load_unit(0).wait()
    for i in range(R):
        plane(0, i)
        if i == 0:
            pl.semaphore_wait(barrier, W + 2)

        @pl.loop(0, W - 1, unroll=9)
        def _(k):
            send_piece_a(0, i, peer_at(k))

    own_a(0).start()
    for u in range(1, 4):
        load_unit(u).wait()

        @pl.loop(0, R)
        def _(i):
            plane(u, i)

        if u == 1:

            @pl.loop(0, W - 1, unroll=9)
            def _(k):
                send_piece_a(1, 0, peer_at(k))

        own_a(u).start()

    for j in range(R):

        @pl.loop(0, W - 1, unroll=9)
        def _(k):
            peer = peer_at(k)
            send_piece_a(2, j, peer)
            send_piece_a(3, j, peer)

    for k in range(6, 14):
        load_table(k).wait()

    sums_g[...] = jnp.zeros_like(sums_g)

    @pl.loop(0, R)
    def _(i):
        kinetic = kinetic_plane(R * me + i)
        for n in range(2):
            shifted = kinetic - energies[0, n]
            real = shifted * raw[2 * n + 1, 0, i]
            imag = shifted * raw[2 * n + 1, 1, i]
            for m in range(2):
                left_real, left_imag = raw[2 * m, 0, i], raw[2 * m, 1, i]
                at = (m * 2 + n) * 2
                sums_g[at] += row_sums(left_real * real + left_imag * imag)
                sums_g[at + 1] += row_sums(left_real * imag - left_imag * real)

    loads_pot.wait()
    loads_pert.wait()
    sums[...] = jnp.zeros_like(sums)

    def columns(n, j):
        at = j * 3 * G
        first = 2 * n * BLOCKS * W
        second = (2 * n + 1) * BLOCKS * W
        orb = spin(table_left(il_h[...], il_l[...], tiles_at(in_a_rows, first + at)), 1.0)
        resp = spin(table_left(il_h[...], il_l[...], tiles_at(in_a_rows, second + at)), 1.0)
        pot_top = pot[j, :, 0:128]
        pert_top = pert[j, :, 0:128]
        pot_end = jnp.concatenate((pot[j, :, 128:G], pot[j, :, 128:G]), axis=1)
        pert_end = jnp.concatenate((pert[j, :, 128:G], pert[j, :, 128:G]), axis=1)
        app = (
            pot_top * resp[0] + pert_top * orb[0],
            pot_top * resp[1] + pert_top * orb[1],
            pot_end * resp[2] + pert_end * orb[2],
        )
        ends = orb[2] * resp[2]
        density = (2.0 * weights[0]) * jnp.concatenate(
            (orb[0] * resp[0] + orb[1] * resp[1], ends + swap64(ends)), axis=1
        )

        def overlap(left, right, slot):
            sums[slot] += row_sums(left[0] * right[0] + left[1] * right[1] + left[2] * right[2])
            sums[slot + 1] += row_sums(
                left[0] * right[1]
                - left[1] * right[0]
                - lane_sign() * left[2] * swap64(right[2])
            )

        if n == 0:
            overlap(orb, app, 0)
            dens[j] = density
            for t in range(3):
                orb_space[j, t] = orb[t]
                app_space[j, t] = app[t]
        else:
            dens[j] = dens[j] + density
            orb_first = [orb_space[j, t] for t in range(3)]
            app_first = [app_space[j, t] for t in range(3)]
            overlap(orb_first, app, 2)
            overlap(orb, app_first, 4)
            overlap(orb, app, 6)
        product = table_left(ol_h[...], ol_l[...], jnp.concatenate(app, axis=1))
        turned = jnp.concatenate(spin(product, -1.0), axis=1)
        back = table_right(turned, bk_h[...], bk_l[...])
        for i in range(R):
            for t in range(3):
                start = (n * BLOCKS + (i * 3 + t) * R + j) * W
                out_r_rows[rows_of(start, W), :] = back[
                    i * W : (i + 1) * W, t * 128 : (t + 1) * 128
                ]

    def piece_r(ref, n, part, who):
        if n == 0:
            return ref.at[n, :, :, who]
        return ref.at[n, :, part, who]

    def send_piece_r(n, part, peer):
        pltpu.make_async_remote_copy(
            src_ref=piece_r(out_r, n, part, peer),
            dst_ref=piece_r(in_r, n, part, me),
            send_sem=send_r.at[n, part],
            recv_sem=recv_r.at[n, part],
            device_id={"pw": peer},
            device_id_type=MESH,
        ).start()

    def own_r(n):
        return pltpu.make_async_copy(
            out_r.at[n, :, :, me], in_r.at[n, :, :, me], load_sem.at[10 + n]
        )

    for i in range(R):
        wait_bytes(piece_a(in_a, 0, i, others), recv_a.at[0, i])
    wait_bytes(piece_a(in_a, 1, 0, others), recv_a.at[1, 0])
    own_a(0).wait()
    own_a(1).wait()

    @pl.loop(0, R)
    def _(j):
        columns(0, j)

    @pl.loop(0, W - 1, unroll=9)
    def _(k):
        send_piece_r(0, 0, peer_at(k))

    own_r(0).start()
    own_a(2).wait()
    own_a(3).wait()

    strips_of = ((0, 2), (2, 1), (3, 2))

    def pool_copy(j, rows):
        strips = pl.ds(*strips_of[j])
        return pltpu.make_async_remote_copy(
            src_ref=fold_mine.at[strips, rows],
            dst_ref=fold_other.at[strips, rows],
            send_sem=send_d.at[j],
            recv_sem=recv_d.at[j],
            device_id={"pool": 1 - pool},
            device_id_type=MESH,
        )

    def mirror_copy(j, rows):
        strips = pl.ds(*strips_of[j])
        return pltpu.make_async_remote_copy(
            src_ref=fold_sum.at[strips, rows],
            dst_ref=fold_mirror.at[strips, rows],
            send_sem=send_d.at[3 + j],
            recv_sem=recv_d.at[3 + j],
            device_id={"pool": 1 - pool, "pw": mirrors[min(j, 1)]},
            device_id_type=MESH,
        )

    def piece_d(ref, j, who):
        first, count = strips_of[j]
        return ref.at[pl.ds(3 * first, 3 * count), who]

    def spread(j):
        first, count = strips_of[j]
        pool_copy(j, kept).wait()
        summed = [
            fold_mine_rows[pl.ds(t * H, H), :] + fold_other_rows[pl.ds(t * H, H), :]
            for t in range(first, first + count)
        ]
        for t in range(count):
            fold_sum_rows[pl.ds((first + t) * H, H), :] = summed[t]
        whole = exact_left(unfold[...], jnp.concatenate(summed, axis=1))
        for t in range(count):
            spread_out_rows[pl.ds((first + t) * G, G), :] = whole[:, t * 128 : (t + 1) * 128]

        @pl.loop(0, 7)
        def _(c):
            mirror_copy(j, pl.ds(c * C, C)).start()
            for k in range(9):
                peer = peer_at(c * 9 + k)
                pltpu.make_async_remote_copy(
                    src_ref=piece_d(spread_out, j, peer),
                    dst_ref=piece_d(spread_in, j, me),
                    send_sem=send_d.at[6 + j],
                    recv_sem=recv_d.at[6 + j],
                    device_id={"pw": peer},
                    device_id_type=MESH,
                ).start()

    lane = lax.broadcasted_iota(jnp.int32, (1, 128), 1)
    for j in range(R):
        for u in (2, 3):
            wait_bytes(piece_a(in_a, u, j, others), recv_a.at[u, j])
        columns(1, j)
        if j == 0:
            strips = (dens[0, :, 0:128], dens[0, :, 128:256])
        elif j == 1:
            strips = (dens[1, :, 0:128],)
        else:
            strips = (
                dens[2, :, 0:128],
                jnp.where(lane < 64, dens[1, :, 128:256], dens[2, :, 128:256]),
            )
        first, count = strips_of[j]
        folded = exact_left(fold[...], jnp.concatenate(strips, axis=1))
        for t in range(count):
            fold_mine_rows[pl.ds((first + t) * H, H), :] = folded[:, t * 128 : (t + 1) * 128]

        @pl.loop(0, 7)
        def _(c):
            pool_copy(j, pl.ds(c * C, C)).start()
            for k in range(9):
                send_piece_r(1, j, peer_at(c * 9 + k))

    own_r(1).start()
    row = jnp.zeros((1, 128), F32)
    for k in range(8):
        one = jnp.sum(sums[k], keepdims=True) + jnp.sum(sums_g[k], keepdims=True)
        row = jnp.where(lane == k, one, row)
    row_out[...] = row
    row_in[me] = row

    @pl.loop(0, W - 1, unroll=9)
    def _(k):
        pltpu.make_async_remote_copy(
            src_ref=row_out,
            dst_ref=row_in.at[me],
            send_sem=send_r.at[2, 0],
            recv_sem=recv_r.at[2, 0],
            device_id={"pw": peer_at(k)},
            device_id_type=MESH,
        ).start()

    for j in range(R):
        spread(j)
    pltpu.make_async_copy(spread_out.at[:, me], spread_in.at[:, me], load_sem.at[12]).start()

    wait_bytes(row_in.at[others], recv_r.at[2, 0])
    totals = jnp.sum(row_in_rows[...], axis=0, keepdims=True) * (1.0 / float(G**3))
    inter = [
        jnp.sum(jnp.where(lane == k, totals, 0.0), axis=1, keepdims=True) for k in range(8)
    ]

    def update(n):
        @pl.loop(0, R)
        def _(i):
            parts = tiles_at(in_r_rows, (n * BLOCKS + i * 9) * W)
            app = spin(table_left(il_h[...], il_l[...], parts), -1.0)
            kinetic = kinetic_plane(R * me + i)
            shifted = kinetic - energies[0, n]
            scale = 1.0 / (1.0 + kinetic)
            real = jnp.concatenate((app[0], app[2][:, :64]), axis=1)
            imag = jnp.concatenate((app[1], swap64(app[2])[:, :64]), axis=1)
            resp_real, resp_imag = raw[2 * n + 1, 0, i], raw[2 * n + 1, 1, i]
            real = real + shifted * resp_real
            imag = imag + shifted * resp_imag
            for m in range(2):
                orb_real, orb_imag = raw[2 * m, 0, i], raw[2 * m, 1, i]
                over_real, over_imag = inter[(m * 2 + n) * 2], inter[(m * 2 + n) * 2 + 1]
                real = real - (over_real * orb_real - over_imag * orb_imag)
                imag = imag - (over_imag * orb_real + over_real * orb_imag)
            new_out[0, n, 0, i] = resp_real - real * scale
            new_out[0, n, 1, i] = resp_imag - imag * scale


    wait_bytes(piece_r(in_r, 0, 0, others), recv_r.at[0, 0])
    own_r(0).wait()
    update(0)

    for j in range(R):
        wait_bytes(piece_r(in_r, 1, j, others), recv_r.at[1, j])
    own_r(1).wait()
    update(1)

    for j in range(R):
        wait_bytes(piece_d(spread_in, j, others), recv_d.at[6 + j])
    pltpu.make_async_copy(spread_out.at[:, me], spread_in.at[:, me], load_sem.at[12]).wait()
    for j in range(R):
        mirror_copy(j, kept).wait()
    own = [fold_sum_rows[pl.ds(t * H, H), :] for t in range(5)]
    seen = [fold_mirror_rows[pl.ds(t * H, H), :] for t in range(5)]
    ends = own[4] + swap64(seen[4])
    local = (
        (own[0] + seen[0], own[1] + seen[1]),
        (own[2] + seen[3], ends),
        (own[3] + seen[2], swap64(ends)),
    )
    for i in range(R):

        def arrived(t):
            return spread_in_rows[pl.ds((t * R + i) * W, W), :]

        top = jnp.concatenate((arrived(0), arrived(2), arrived(3)), axis=0)
        pair = arrived(4)
        end = jnp.concatenate((arrived(1), pair, swap64(pair)), axis=0)
        total = exact_left(merge[...], jnp.concatenate((top, end), axis=1)) + exact_left(
            expand[...], jnp.concatenate(local[i], axis=1)
        )
        dens_out[i] = total[:, :G] * 0.125

    for j in range(R):
        for u in (0, 2, 3):
            wait_bytes(piece_a(out_a, u, j, others), send_a.at[u, j])
        wait_bytes(piece_r(out_r, 1, j, others), send_r.at[1, j])
    wait_bytes(piece_a(out_a, 1, 0, others), send_a.at[1, 0])
    wait_bytes(piece_r(out_r, 0, 0, others), send_r.at[0, 0])
    wait_bytes(row_in.at[others], send_r.at[2, 0])
    for j in range(R):
        wait_bytes(piece_d(spread_out, j, others), send_d.at[6 + j])


def store(new_vmem, dens_vmem, new_hbm, dens_hbm, sem):
    copies = [
        pltpu.make_async_copy(new_vmem.at[0, n, c], new_hbm.at[0, n, c], sem.at[2 * n + c])
        for n in range(2)
        for c in range(2)
    ]
    copies.append(pltpu.make_async_copy(dens_vmem, dens_hbm, sem.at[4]))
    for copy in copies:
        copy.start()
    for copy in copies:
        copy.wait()


def in_hbm(array):
    return pltpu.with_memory_space_constraint(array, pltpu.HBM)


def body(orbitals, responses, energies, weights, potential, perturbation):
    held = [in_hbm(jnp.asarray(table)) for table in tables()]
    anywhere = pl.BlockSpec(memory_space=pl.ANY)
    scalar = pl.BlockSpec(memory_space=pltpu.SMEM)
    vmem, dma = pltpu.VMEM, pltpu.SemaphoreType.DMA
    results = pl.pallas_call(
        kernel,
        out_shape=(
            pltpu.VMEM((1, 2, 2, R, G, G), F32),
            pltpu.VMEM((R, G, G), F32),
        ),
        in_specs=[anywhere] * 4 + [scalar] * 2 + [anywhere] * len(held),
        out_specs=(pl.BlockSpec(memory_space=pltpu.VMEM),) * 2,
        scratch_shapes=[vmem(table.shape, BF16) for table in held]
        + [
            vmem((4, 2, R, G, G), F32),
            vmem((R, G, G), F32),
            vmem((R, G, G), F32),
            vmem((4, 9, R, W, 1, 128), F32),
            vmem((4, 9, R, W, 1, 128), F32),
            vmem((2, 9, R, W, 1, 128), F32),
            vmem((2, 9, R, W, 1, 128), F32),
            vmem((R, 3, G, 128), F32),
            vmem((R, 3, G, 128), F32),
            vmem((R, G, 256), F32),
            vmem((5, H, 1, 128), F32),
            vmem((5, H, 1, 128), F32),
            vmem((5, H, 1, 128), F32),
            vmem((5, H, 1, 128), F32),
            vmem((15, W, 1, 128), F32),
            vmem((15, W, 1, 128), F32),
            vmem((8, 8, 128), F32),
            vmem((8, 8, G), F32),
            vmem((1, 128), F32),
            vmem((W, 1, 128), F32),
            dma((13,)),
            dma((14,)),
            dma((4, R)),
            dma((4, R)),
            dma((3, R)),
            dma((3, R)),
            dma((9,)),
            dma((9,)),
        ],
        compiler_params=pltpu.CompilerParams(
            collective_id=0, has_side_effects=True, vmem_limit_bytes=56 * 2**20
        ),
    )(
        in_hbm(orbitals),
        in_hbm(responses),
        in_hbm(jnp.transpose(potential, (1, 0, 2))),
        in_hbm(jnp.transpose(perturbation, (1, 0, 2))),
        energies,
        weights,
        *held,
    )
    return pl.pallas_call(
        store,
        out_shape=(
            jax.ShapeDtypeStruct((1, 2, 2, R, G, G), F32),
            jax.ShapeDtypeStruct((R, G, G), F32),
        ),
        in_specs=[pl.BlockSpec(memory_space=pltpu.VMEM)] * 2,
        out_specs=(anywhere, anywhere),
        scratch_shapes=[dma((5,))],
    )(*(pltpu.with_memory_space_constraint(result, pltpu.VMEM) for result in results))


def solution(mesh):
    placed = (
        P("pool", None, None, "pw", None, None),
        P("pool", None, None, "pw", None, None),
        P("pool", None),
        P("pool"),
        P(None, "pw", None),
        P(None, "pw", None),
    )
    return jax.shard_map(
        body,
        mesh=mesh,
        in_specs=placed,
        out_specs=(P("pool", None, None, "pw", None, None), P("pw", None, None)),
        check_vma=False,
    )
```

```python
import functools
import math

import jax
import jax.numpy as jnp
import ml_dtypes
import numpy as np
from jax import lax
from jax.experimental import pallas as pl
from jax.experimental.pallas import tpu as pltpu
from jax.sharding import PartitionSpec as P

RECIPROCAL_SQUARE = 0.023428
G = 192
W = 64
R = 3
H = 104
C = 14
K = 7 * C
BLOCKS = 27
MESH = pl.DeviceIdType.MESH
F32 = jnp.float32
BF16 = jnp.bfloat16


def halves(table):
    high = table.astype(ml_dtypes.bfloat16)
    low = (table - high.astype(np.float64)).astype(ml_dtypes.bfloat16)
    return [high, low]


def tables():
    index = np.arange(G)
    angles = (np.outer(index, index) % G) * (2.0 * math.pi / G)
    cosine = np.cos(angles) / math.sqrt(G)
    sine = np.sin(angles) / math.sqrt(G)
    spread = np.array([R * (s % W) + s // W for s in range(G)])

    def packed(left, right):
        return np.concatenate(
            (left[:, :128], right[:, :128], left[:, 128:], right[:, 128:]), axis=1
        )

    out_left = np.concatenate((cosine[spread], sine[spread]), axis=0)
    in_left = np.concatenate((cosine[:, spread], sine[:, spread]), axis=0)
    right_real = packed(cosine, sine)
    right_imag = packed(-sine, cosine)
    back_real = packed(cosine, -sine)
    back_imag = packed(sine, cosine)
    back = np.concatenate(
        (back_real[:128], back_imag[:128], back_real[128:], back_imag[128:]), axis=0
    )
    fold = np.zeros((H, G))
    unfold = np.zeros((G, H))
    merge = np.zeros((G, G))
    expand = np.zeros((G, H))
    for a in range(H):
        fold[a, a] += 1.0
        fold[a, -a % G] += 1.0
    for s in range(G):
        a = spread[s]
        unfold[s, min(a, G - a)] = 1.0
        merge[a, s] += 1.0
        merge[-a % G, s] += 1.0
        expand[s, min(s, G - s)] = 1.0
    held = []
    for table in (right_real, right_imag, out_left, in_left, back):
        held += halves(table)
    return held + [m.astype(ml_dtypes.bfloat16) for m in (fold, unfold, merge, expand)]


def split(values):
    high = values.astype(BF16)
    return high, (values - high.astype(F32)).astype(BF16)


def dot(left, right):
    return jnp.dot(left, right, preferred_element_type=F32)


def table_left(high, low, values):
    top, rest = split(values)
    return dot(high, top) + (dot(high, rest) + dot(low, top))


def table_right(values, high, low):
    top, rest = split(values)
    return dot(top, high) + (dot(rest, high) + dot(top, low))


def exact_left(table, values):
    top, rest = split(values)
    last = (values - top.astype(F32) - rest.astype(F32)).astype(BF16)
    return dot(table, top) + (dot(table, rest) + dot(table, last))


def swap64(values):
    return pltpu.roll(values, 64, axis=1)


def lane_sign():
    return jnp.where(lax.broadcasted_iota(jnp.int32, (1, 128), 1) < 64, -1.0, 1.0).astype(F32)


def spin(product, sign):
    cos_part, sin_part = product[:G], product[G:]
    return (
        cos_part[:, :128] - sign * sin_part[:, 128:256],
        cos_part[:, 128:256] + sign * sin_part[:, :128],
        cos_part[:, 256:] + (sign * lane_sign()) * swap64(sin_part[:, 256:]),
    )


def rows_of(start, count):
    if isinstance(start, int):
        return pl.ds(start, count)
    return pl.ds(pl.multiple_of(start, 8), count)


def tiles_at(view, start):
    return jnp.concatenate([view[rows_of(start + t * G, G), :] for t in range(3)], axis=1)


def row_sums(values):
    total = values[0:8]
    for s in range(8, G, 8):
        total = total + values[s : s + 8]
    return total


def squared_freq(index):
    freq = jnp.where(index < G // 2, index, index - G).astype(F32)
    return freq * freq


def kinetic_plane(row):
    plane = squared_freq(lax.broadcasted_iota(jnp.int32, (G, G), 0))
    plane = plane + squared_freq(lax.broadcasted_iota(jnp.int32, (G, G), 1))
    return (0.5 * RECIPROCAL_SQUARE) * (squared_freq(row) + plane)


def kernel(
    orb_hbm, resp_hbm, pot_hbm, pert_hbm, energies, weights, *refs
):
    table_hbm = refs[:14]
    new_out, dens_out = refs[14:16]
    tables_in = refs[16:30]
    (
        raw, pot, pert, out_a, in_a, out_r, in_r, orb_space, app_space, dens,
        fold_mine, fold_other, fold_sum, fold_mirror, spread_out, spread_in,
        sums, sums_g, row_out, row_in,
        load_sem, table_sem, send_a, recv_a, send_r, recv_r, send_d, recv_d,
    ) = refs[30:]
    (wr_h, wr_l, wi_h, wi_l, ol_h, ol_l, il_h, il_l, bk_h, bk_l, fold, unfold, merge, expand) = tables_in

    me = lax.axis_index("pw")
    pool = lax.axis_index("pool")

    def load_table(k):
        return pltpu.make_async_copy(table_hbm[k], tables_in[k], table_sem.at[k])

    def load_unit(u):
        source = orb_hbm if u % 2 == 0 else resp_hbm
        return pltpu.make_async_copy(source.at[0, u // 2], raw.at[u], load_sem.at[u])

    loads_pot = pltpu.make_async_copy(pot_hbm, pot, load_sem.at[4])
    loads_pert = pltpu.make_async_copy(pert_hbm, pert, load_sem.at[5])
    for k in range(4):
        load_table(k).start()
    load_unit(0).start()
    for k in range(4, 6):
        load_table(k).start()
    out_a_rows = out_a.reshape(4 * BLOCKS * W, 128)
    in_a_rows = in_a.reshape(4 * BLOCKS * W, 128)
    out_r_rows = out_r.reshape(2 * BLOCKS * W, 128)
    in_r_rows = in_r.reshape(2 * BLOCKS * W, 128)
    spread_out_rows = spread_out.reshape(15 * W, 128)
    spread_in_rows = spread_in.reshape(15 * W, 128)
    row_in_rows = row_in.reshape(W, 128)
    fold_mine_rows = fold_mine.reshape(5 * H, 128)
    fold_other_rows = fold_other.reshape(5 * H, 128)
    fold_sum_rows = fold_sum.reshape(5 * H, 128)
    fold_mirror_rows = fold_mirror.reshape(5 * H, 128)

    for t in range(5):
        fold_other_rows[pl.ds(t * H + H - 8, 8), :] = jnp.zeros((8, 128), F32)
        fold_mirror_rows[pl.ds(t * H + H - 8, 8), :] = jnp.zeros((8, 128), F32)
    kept = pl.ds(0, K)
    mirrors = ((W - me) % W, W - 1 - me)

    barrier = pltpu.get_barrier_semaphore()

    def peer_at(k):
        return me ^ (1 + (k * 37 + 11) % (W - 1))

    @pl.loop(0, W - 1, unroll=9)
    def _(k):
        pl.semaphore_signal(barrier, inc=1, device_id={"pw": peer_at(k)}, device_id_type=MESH)

    for who in (me, *mirrors):
        pl.semaphore_signal(
            barrier, inc=1, device_id={"pool": 1 - pool, "pw": who}, device_id_type=MESH
        )

    for u in range(1, 4):
        load_unit(u).start()
    for k in range(6, 14):
        load_table(k).start()
    loads_pot.start()
    loads_pert.start()

    for k in range(6):
        load_table(k).wait()

    def piece_a(ref, u, part, who):
        if u == 0:
            return ref.at[u, :, part, who]
        if u == 1:
            return ref.at[u, :, :, who]
        return ref.at[u, pl.ds(3 * part, 3), :, who]

    def send_piece_a(u, part, peer):
        pltpu.make_async_remote_copy(
            src_ref=piece_a(out_a, u, part, peer),
            dst_ref=piece_a(in_a, u, part, me),
            send_sem=send_a.at[u, part],
            recv_sem=recv_a.at[u, part],
            device_id={"pw": peer},
            device_id_type=MESH,
        ).start()

    def wait_bytes(ref, sem):
        pltpu.make_async_copy(ref, ref, sem).wait()

    others = pl.ds(0, W - 1)

    def own_a(u):
        return pltpu.make_async_copy(
            out_a.at[u, :, :, me], in_a.at[u, :, :, me], load_sem.at[6 + u]
        )

    def plane(u, i):
        planes = table_right(raw[u, 0, i], wr_h[...], wr_l[...]) + table_right(
            raw[u, 1, i], wi_h[...], wi_l[...]
        )
        parts = spin(table_left(ol_h[...], ol_l[...], planes), 1.0)
        for j in range(R):
            for t in range(3):
                start = (u * BLOCKS + (j * 3 + t) * R + i) * W
                out_a_rows[rows_of(start, W), :] = parts[t][j * W : (j + 1) * W]

    load_unit(0).wait()
    for i in range(R):
        plane(0, i)
        if i == 0:
            pl.semaphore_wait(barrier, W + 2)

        @pl.loop(0, W - 1, unroll=9)
        def _(k):
            send_piece_a(0, i, peer_at(k))

    own_a(0).start()
    for u in range(1, 4):
        load_unit(u).wait()

        @pl.loop(0, R)
        def _(i):
            plane(u, i)

        if u == 1:

            @pl.loop(0, W - 1, unroll=9)
            def _(k):
                send_piece_a(1, 0, peer_at(k))

        own_a(u).start()

    for j in range(R):

        @pl.loop(0, W - 1, unroll=9)
        def _(k):
            peer = peer_at(k)
            send_piece_a(2, j, peer)
            send_piece_a(3, j, peer)

    for k in range(6, 14):
        load_table(k).wait()

    sums_g[...] = jnp.zeros_like(sums_g)

    @pl.loop(0, R)
    def _(i):
        kinetic = kinetic_plane(R * me + i)
        for n in range(2):
            shifted = kinetic - energies[0, n]
            real = shifted * raw[2 * n + 1, 0, i]
            imag = shifted * raw[2 * n + 1, 1, i]
            for m in range(2):
                left_real, left_imag = raw[2 * m, 0, i], raw[2 * m, 1, i]
                at = (m * 2 + n) * 2
                sums_g[at] += row_sums(left_real * real + left_imag * imag)
                sums_g[at + 1] += row_sums(left_real * imag - left_imag * real)

    loads_pot.wait()
    loads_pert.wait()
    sums[...] = jnp.zeros_like(sums)

    def columns(n, j):
        at = j * 3 * G
        first = 2 * n * BLOCKS * W
        second = (2 * n + 1) * BLOCKS * W
        orb = spin(table_left(il_h[...], il_l[...], tiles_at(in_a_rows, first + at)), 1.0)
        resp = spin(table_left(il_h[...], il_l[...], tiles_at(in_a_rows, second + at)), 1.0)
        pot_top = pot[j, :, 0:128]
        pert_top = pert[j, :, 0:128]
        pot_end = jnp.concatenate((pot[j, :, 128:G], pot[j, :, 128:G]), axis=1)
        pert_end = jnp.concatenate((pert[j, :, 128:G], pert[j, :, 128:G]), axis=1)
        app = (
            pot_top * resp[0] + pert_top * orb[0],
            pot_top * resp[1] + pert_top * orb[1],
            pot_end * resp[2] + pert_end * orb[2],
        )
        ends = orb[2] * resp[2]
        density = (2.0 * weights[0]) * jnp.concatenate(
            (orb[0] * resp[0] + orb[1] * resp[1], ends + swap64(ends)), axis=1
        )

        def overlap(left, right, slot):
            sums[slot] += row_sums(left[0] * right[0] + left[1] * right[1] + left[2] * right[2])
            sums[slot + 1] += row_sums(
                left[0] * right[1]
                - left[1] * right[0]
                - lane_sign() * left[2] * swap64(right[2])
            )

        if n == 0:
            overlap(orb, app, 0)
            dens[j] = density
            for t in range(3):
                orb_space[j, t] = orb[t]
                app_space[j, t] = app[t]
        else:
            dens[j] = dens[j] + density
            orb_first = [orb_space[j, t] for t in range(3)]
            app_first = [app_space[j, t] for t in range(3)]
            overlap(orb_first, app, 2)
            overlap(orb, app_first, 4)
            overlap(orb, app, 6)
        product = table_left(ol_h[...], ol_l[...], jnp.concatenate(app, axis=1))
        turned = jnp.concatenate(spin(product, -1.0), axis=1)
        back = table_right(turned, bk_h[...], bk_l[...])
        for i in range(R):
            for t in range(3):
                start = (n * BLOCKS + (i * 3 + t) * R + j) * W
                out_r_rows[rows_of(start, W), :] = back[
                    i * W : (i + 1) * W, t * 128 : (t + 1) * 128
                ]

    def piece_r(ref, n, part, who):
        if n == 0:
            return ref.at[n, :, :, who]
        return ref.at[n, :, part, who]

    def send_piece_r(n, part, peer):
        pltpu.make_async_remote_copy(
            src_ref=piece_r(out_r, n, part, peer),
            dst_ref=piece_r(in_r, n, part, me),
            send_sem=send_r.at[n, part],
            recv_sem=recv_r.at[n, part],
            device_id={"pw": peer},
            device_id_type=MESH,
        ).start()

    def own_r(n):
        return pltpu.make_async_copy(
            out_r.at[n, :, :, me], in_r.at[n, :, :, me], load_sem.at[10 + n]
        )

    for i in range(R):
        wait_bytes(piece_a(in_a, 0, i, others), recv_a.at[0, i])
    wait_bytes(piece_a(in_a, 1, 0, others), recv_a.at[1, 0])
    own_a(0).wait()
    own_a(1).wait()

    @pl.loop(0, R)
    def _(j):
        columns(0, j)

    @pl.loop(0, W - 1, unroll=9)
    def _(k):
        send_piece_r(0, 0, peer_at(k))

    own_r(0).start()
    own_a(2).wait()
    own_a(3).wait()

    strips_of = ((0, 2), (2, 1), (3, 2))

    def pool_copy(j, rows):
        strips = pl.ds(*strips_of[j])
        return pltpu.make_async_remote_copy(
            src_ref=fold_mine.at[strips, rows],
            dst_ref=fold_other.at[strips, rows],
            send_sem=send_d.at[j],
            recv_sem=recv_d.at[j],
            device_id={"pool": 1 - pool},
            device_id_type=MESH,
        )

    def mirror_copy(j, rows):
        strips = pl.ds(*strips_of[j])
        return pltpu.make_async_remote_copy(
            src_ref=fold_sum.at[strips, rows],
            dst_ref=fold_mirror.at[strips, rows],
            send_sem=send_d.at[3 + j],
            recv_sem=recv_d.at[3 + j],
            device_id={"pool": 1 - pool, "pw": mirrors[min(j, 1)]},
            device_id_type=MESH,
        )

    def spread(j):
        first, count = strips_of[j]
        pool_copy(j, kept).wait()
        summed = [
            fold_mine_rows[pl.ds(t * H, H), :] + fold_other_rows[pl.ds(t * H, H), :]
            for t in range(first, first + count)
        ]
        for t in range(count):
            fold_sum_rows[pl.ds((first + t) * H, H), :] = summed[t]
        whole = exact_left(unfold[...], jnp.concatenate(summed, axis=1))
        for t in range(count):
            spread_out_rows[pl.ds((first + t) * G, G), :] = whole[:, t * 128 : (t + 1) * 128]

    lane = lax.broadcasted_iota(jnp.int32, (1, 128), 1)
    for j in range(R):
        for u in (2, 3):
            wait_bytes(piece_a(in_a, u, j, others), recv_a.at[u, j])
        columns(1, j)
        if j == 0:
            strips = (dens[0, :, 0:128], dens[0, :, 128:256])
        elif j == 1:
            strips = (dens[1, :, 0:128],)
        else:
            strips = (
                dens[2, :, 0:128],
                jnp.where(lane < 64, dens[1, :, 128:256], dens[2, :, 128:256]),
            )
        first, count = strips_of[j]
        folded = exact_left(fold[...], jnp.concatenate(strips, axis=1))
        for t in range(count):
            fold_mine_rows[pl.ds((first + t) * H, H), :] = folded[:, t * 128 : (t + 1) * 128]

        @pl.loop(0, 7)
        def _(c):
            pool_copy(j, pl.ds(c * C, C)).start()
            for k in range(9):
                send_piece_r(1, j, peer_at(c * 9 + k))

    own_r(1).start()
    row = jnp.zeros((1, 128), F32)
    for k in range(8):
        one = jnp.sum(sums[k], keepdims=True) + jnp.sum(sums_g[k], keepdims=True)
        row = jnp.where(lane == k, one, row)
    row_out[...] = row
    row_in[me] = row

    @pl.loop(0, W - 1, unroll=9)
    def _(k):
        pltpu.make_async_remote_copy(
            src_ref=row_out,
            dst_ref=row_in.at[me],
            send_sem=send_r.at[2, 0],
            recv_sem=recv_r.at[2, 0],
            device_id={"pw": peer_at(k)},
            device_id_type=MESH,
        ).start()

    for j in range(R):
        spread(j)

    @pl.loop(0, 7)
    def _(c):
        for j in range(R):
            mirror_copy(j, pl.ds(c * C, C)).start()
        for k in range(9):
            peer = peer_at(c * 9 + k)
            pltpu.make_async_remote_copy(
                src_ref=spread_out.at[:, peer],
                dst_ref=spread_in.at[:, me],
                send_sem=send_d.at[6],
                recv_sem=recv_d.at[6],
                device_id={"pw": peer},
                device_id_type=MESH,
            ).start()

    pltpu.make_async_copy(spread_out.at[:, me], spread_in.at[:, me], load_sem.at[12]).start()

    wait_bytes(row_in.at[others], recv_r.at[2, 0])
    totals = jnp.sum(row_in_rows[...], axis=0, keepdims=True) * (1.0 / float(G**3))
    inter = [
        jnp.sum(jnp.where(lane == k, totals, 0.0), axis=1, keepdims=True) for k in range(8)
    ]

    def update(n):
        @pl.loop(0, R)
        def _(i):
            parts = tiles_at(in_r_rows, (n * BLOCKS + i * 9) * W)
            app = spin(table_left(il_h[...], il_l[...], parts), -1.0)
            kinetic = kinetic_plane(R * me + i)
            shifted = kinetic - energies[0, n]
            scale = 1.0 / (1.0 + kinetic)
            real = jnp.concatenate((app[0], app[2][:, :64]), axis=1)
            imag = jnp.concatenate((app[1], swap64(app[2])[:, :64]), axis=1)
            resp_real, resp_imag = raw[2 * n + 1, 0, i], raw[2 * n + 1, 1, i]
            real = real + shifted * resp_real
            imag = imag + shifted * resp_imag
            for m in range(2):
                orb_real, orb_imag = raw[2 * m, 0, i], raw[2 * m, 1, i]
                over_real, over_imag = inter[(m * 2 + n) * 2], inter[(m * 2 + n) * 2 + 1]
                real = real - (over_real * orb_real - over_imag * orb_imag)
                imag = imag - (over_imag * orb_real + over_real * orb_imag)
            new_out[0, n, 0, i] = resp_real - real * scale
            new_out[0, n, 1, i] = resp_imag - imag * scale


    wait_bytes(piece_r(in_r, 0, 0, others), recv_r.at[0, 0])
    own_r(0).wait()
    update(0)

    for j in range(R):
        wait_bytes(piece_r(in_r, 1, j, others), recv_r.at[1, j])
    own_r(1).wait()
    update(1)

    wait_bytes(spread_in.at[:, others], recv_d.at[6])
    pltpu.make_async_copy(spread_out.at[:, me], spread_in.at[:, me], load_sem.at[12]).wait()
    for j in range(R):
        mirror_copy(j, kept).wait()
    own = [fold_sum_rows[pl.ds(t * H, H), :] for t in range(5)]
    seen = [fold_mirror_rows[pl.ds(t * H, H), :] for t in range(5)]
    ends = own[4] + swap64(seen[4])
    local = (
        (own[0] + seen[0], own[1] + seen[1]),
        (own[2] + seen[3], ends),
        (own[3] + seen[2], swap64(ends)),
    )
    for i in range(R):

        def arrived(t):
            return spread_in_rows[pl.ds((t * R + i) * W, W), :]

        top = jnp.concatenate((arrived(0), arrived(2), arrived(3)), axis=0)
        pair = arrived(4)
        end = jnp.concatenate((arrived(1), pair, swap64(pair)), axis=0)
        total = exact_left(merge[...], jnp.concatenate((top, end), axis=1)) + exact_left(
            expand[...], jnp.concatenate(local[i], axis=1)
        )
        dens_out[i] = total[:, :G] * 0.125

    for j in range(R):
        for u in (0, 2, 3):
            wait_bytes(piece_a(out_a, u, j, others), send_a.at[u, j])
        wait_bytes(piece_r(out_r, 1, j, others), send_r.at[1, j])
    wait_bytes(piece_a(out_a, 1, 0, others), send_a.at[1, 0])
    wait_bytes(piece_r(out_r, 0, 0, others), send_r.at[0, 0])
    wait_bytes(row_in.at[others], send_r.at[2, 0])
    wait_bytes(spread_out.at[:, others], send_d.at[6])


def store(new_vmem, dens_vmem, new_hbm, dens_hbm, sem):
    copies = [
        pltpu.make_async_copy(new_vmem.at[0, n, c], new_hbm.at[0, n, c], sem.at[2 * n + c])
        for n in range(2)
        for c in range(2)
    ]
    copies.append(pltpu.make_async_copy(dens_vmem, dens_hbm, sem.at[4]))
    for copy in copies:
        copy.start()
    for copy in copies:
        copy.wait()


def in_hbm(array):
    return pltpu.with_memory_space_constraint(array, pltpu.HBM)


def body(orbitals, responses, energies, weights, potential, perturbation):
    held = [in_hbm(jnp.asarray(table)) for table in tables()]
    anywhere = pl.BlockSpec(memory_space=pl.ANY)
    scalar = pl.BlockSpec(memory_space=pltpu.SMEM)
    vmem, dma = pltpu.VMEM, pltpu.SemaphoreType.DMA
    results = pl.pallas_call(
        kernel,
        out_shape=(
            pltpu.VMEM((1, 2, 2, R, G, G), F32),
            pltpu.VMEM((R, G, G), F32),
        ),
        in_specs=[anywhere] * 4 + [scalar] * 2 + [anywhere] * len(held),
        out_specs=(pl.BlockSpec(memory_space=pltpu.VMEM),) * 2,
        scratch_shapes=[vmem(table.shape, BF16) for table in held]
        + [
            vmem((4, 2, R, G, G), F32),
            vmem((R, G, G), F32),
            vmem((R, G, G), F32),
            vmem((4, 9, R, W, 1, 128), F32),
            vmem((4, 9, R, W, 1, 128), F32),
            vmem((2, 9, R, W, 1, 128), F32),
            vmem((2, 9, R, W, 1, 128), F32),
            vmem((R, 3, G, 128), F32),
            vmem((R, 3, G, 128), F32),
            vmem((R, G, 256), F32),
            vmem((5, H, 1, 128), F32),
            vmem((5, H, 1, 128), F32),
            vmem((5, H, 1, 128), F32),
            vmem((5, H, 1, 128), F32),
            vmem((15, W, 1, 128), F32),
            vmem((15, W, 1, 128), F32),
            vmem((8, 8, 128), F32),
            vmem((8, 8, G), F32),
            vmem((1, 128), F32),
            vmem((W, 1, 128), F32),
            dma((13,)),
            dma((14,)),
            dma((4, R)),
            dma((4, R)),
            dma((3, R)),
            dma((3, R)),
            dma((7,)),
            dma((7,)),
        ],
        compiler_params=pltpu.CompilerParams(
            collective_id=0, has_side_effects=True, vmem_limit_bytes=56 * 2**20
        ),
    )(
        in_hbm(orbitals),
        in_hbm(responses),
        in_hbm(jnp.transpose(potential, (1, 0, 2))),
        in_hbm(jnp.transpose(perturbation, (1, 0, 2))),
        energies,
        weights,
        *held,
    )
    return pl.pallas_call(
        store,
        out_shape=(
            jax.ShapeDtypeStruct((1, 2, 2, R, G, G), F32),
            jax.ShapeDtypeStruct((R, G, G), F32),
        ),
        in_specs=[pl.BlockSpec(memory_space=pltpu.VMEM)] * 2,
        out_specs=(anywhere, anywhere),
        scratch_shapes=[dma((5,))],
    )(*(pltpu.with_memory_space_constraint(result, pltpu.VMEM) for result in results))


def solution(mesh):
    placed = (
        P("pool", None, None, "pw", None, None),
        P("pool", None, None, "pw", None, None),
        P("pool", None),
        P("pool"),
        P(None, "pw", None),
        P(None, "pw", None),
    )
    return jax.shard_map(
        body,
        mesh=mesh,
        in_specs=placed,
        out_specs=(P("pool", None, None, "pw", None, None), P("pw", None, None)),
        check_vma=False,
    )
```
